32 devices in a mesh: gx: 4 (over z), gy: 8 (over y, x, core).
Axes of the slice: x: 2, y: 2, z: 4, core: 2. Of those that a mesh axis runs over, the one named last changes fastest.
Arguments:
- right_side: float32 [128, 256, 128], P('gx', 'gy'), may hold values from -6 to 6
- permittivity: float32 [128, 256, 128], P('gx', 'gy'), may hold values from 0.175 to 5.6
Outputs:
- potential: float32 [128, 256, 128], P('gx', 'gy')
The draws below stay inside these ranges and needn't reach their ends.
All inputs are finite; a program needn't handle non-finite values.
Results may differ from the reference program's by a relative error of at most 0.00002.
Values sent between devices are 32-bit elements; how exact they have to be, the bound alone decides.
A program may use at most 192 MiB of HBM per device.

```python
import jax
import jax.numpy as jnp

LEVELS = 5
SMOOTH = 2
COARSE_SWEEPS = 12
NX = 128
NY = 256
NZ = 128


def draw_right_side(key, part):
    grid_shape = (NX, NY, NZ)
    return jnp.clip(0.75 + jax.random.normal(key, grid_shape, jnp.float32), -6.0, 6.0)


def draw_permittivity(key, part):
    grid_shape = (NX, NY, NZ)
    block_cells = 2 ** (LEVELS - 1)
    index_x = jnp.arange(NX, dtype=jnp.int32) // block_cells
    index_z = jnp.arange(NZ, dtype=jnp.int32) // block_cells
    fibre_on = (index_x[:, None, None] + index_z[None, None, :]) % 2 == 0
    background = jnp.where(fibre_on, jnp.float32(4.0), jnp.float32(0.25))
    factor = jnp.exp(jax.random.uniform(key, grid_shape, jnp.float32, jnp.log(0.7), jnp.log(1.4)))
    return jnp.broadcast_to(background, grid_shape) * factor


def setup_inputs(seed: int = 0) -> dict:
    streams_of = jax.random.split(jax.random.key(seed), 3)
    right_side = draw_right_side(jax.random.fold_in(streams_of[2], 71), 0)
    permittivity = draw_permittivity(jax.random.fold_in(streams_of[2], 71), 0)
    return {"right_side": right_side, "permittivity": permittivity}


def restrict(values):
    rows_x, rows_y, rows_z = values.shape
    return values.reshape(rows_x // 2, 2, rows_y // 2, 2, rows_z // 2, 2).sum(axis=(1, 3, 5)) * 0.125


def inject(values):
    rows_x, rows_y, rows_z = values.shape
    spread_out = jnp.broadcast_to(values[:, None, :, None, :, None], (rows_x, 2, rows_y, 2, rows_z, 2))
    return spread_out.reshape(2 * rows_x, 2 * rows_y, 2 * rows_z)


def side_values(extended):
    return (extended[2:, 1:-1, 1:-1], extended[:-2, 1:-1, 1:-1], extended[1:-1, 2:, 1:-1],
            extended[1:-1, :-2, 1:-1], extended[1:-1, 1:-1, 2:], extended[1:-1, 1:-1, :-2])


def face_weights(permit, extended, level_scale):
    return tuple(level_scale * 2.0 * permit * neighbour / (permit + neighbour) for neighbour in side_values(extended))


def beside_sum(weights, extended):
    values = side_values(extended)
    running = weights[0] * values[0]
    for k in range(1, 6):
        running = running + weights[k] * values[k]
    return running


def weight_total(weights):
    running = weights[0]
    for k in range(1, 6):
        running = running + weights[k]
    return running


def colours(rows_x, rows_y, rows_z, offset_x, offset_y):
    index_x = offset_x + jnp.arange(rows_x, dtype=jnp.int32)
    index_y = offset_y + jnp.arange(rows_y, dtype=jnp.int32)
    index_z = jnp.arange(rows_z, dtype=jnp.int32)
    return (index_x[:, None, None] + index_y[None, :, None] + index_z[None, None, :]) % 2


def pad_permit(permit):
    edged = jnp.pad(permit, ((1, 1), (1, 1), (0, 0)), mode="edge")
    return jnp.pad(edged, ((0, 0), (0, 0), (1, 1)))


def smooth(potential, source, weights, weight_sum, parity, sweeps):
    for sweep_index in range(sweeps):
        for colour in range(2):
            updated = (source + beside_sum(weights, jnp.pad(potential, 1))) / weight_sum
            potential = jnp.where(parity == colour, updated, potential)
    return potential


def cycle(level_index, source, permit):
    level_scale = 0.25 ** level_index
    weights = face_weights(permit, pad_permit(permit), level_scale)
    weight_sum = weight_total(weights)
    rows_x, rows_y, rows_z = source.shape
    parity = colours(rows_x, rows_y, rows_z, 0, 0)
    zeros_start = jnp.zeros(source.shape, jnp.float32)
    if level_index == LEVELS - 1:
        return smooth(zeros_start, source, weights, weight_sum, parity, COARSE_SWEEPS)
    potential = smooth(zeros_start, source, weights, weight_sum, parity, SMOOTH)
    residual_field = source - (weight_sum * potential - beside_sum(weights, jnp.pad(potential, 1)))
    correction = cycle(level_index + 1, restrict(residual_field), restrict(permit))
    potential = potential + inject(correction)
    return smooth(potential, source, weights, weight_sum, parity, SMOOTH)


def reference(right_side, permittivity):
    return cycle(0, right_side, permittivity)
```

```python
import functools

import jax
import jax.numpy as jnp
from jax import lax
from jax.experimental import pallas as pl
from jax.experimental.pallas import tpu as pltpu
from jax.sharding import PartitionSpec as P

LEVELS = 5
SMOOTH = 2
COARSE_SWEEPS = 12
MESH = pl.DeviceIdType.MESH
F32 = jnp.float32


DIRS = [(dx, dy) for dx in (-1, 0, 1) for dy in (-1, 0, 1) if (dx, dy) != (0, 0)]
DIRS.sort(key=lambda d: (d[0] == 0, d[1] != 0))


class Level:
    pass


def iota(shape, dim):
    return lax.broadcasted_iota(jnp.int32, shape, dim)


def even_mask(rows, lanes):
    return (iota((rows, lanes), 0) + iota((rows, lanes), 1)) % 2 == 0


def roll(x, shift, axis):
    return pltpu.roll(x, shift % x.shape[axis], axis)


def sum_lanes(x, lanes):
    pick = jnp.where(iota((lanes, lanes), 0) // 2 == iota((lanes, lanes), 1), F32(0.125), F32(0.0))
    return jnp.dot(x, pick, precision=lax.Precision.HIGHEST, preferred_element_type=F32)


def spread_lanes(x, lanes):
    pick = jnp.where(iota((lanes, lanes), 0) == iota((lanes, lanes), 1) // 2, F32(1.0), F32(0.0))
    return jnp.dot(x, pick, precision=lax.Precision.HIGHEST, preferred_element_type=F32)


def put_rows(tmp, t, values):
    for h in range(tmp.shape[1]):
        tmp[t, h, 0 : values.shape[-2], :] = values[..., h * 128 : h * 128 + 128]


def get_row(tmp, t, high):
    tiles = [tmp[t, h, 0:high, :] for h in range(tmp.shape[1])]
    return tiles[0] if len(tiles) == 1 else jnp.concatenate(tiles, axis=-1)


def get_strided(tmp, rows, count, first):
    tiles = [tmp[0:rows, h, pl.ds(first, count, 2), :] for h in range(tmp.shape[1])]
    return tiles[0] if len(tiles) == 1 else jnp.concatenate(tiles, axis=-1)


def restrict(tmp, rows, high):
    lanes = tmp.shape[1] * 128
    both = get_strided(tmp, rows, high // 2, 0) + get_strided(tmp, rows, high // 2, 1)
    flat = both.reshape(rows * (high // 2), lanes)
    return sum_lanes(flat, lanes).reshape(rows, high // 2, lanes)


def spread(tmp, coarse):
    rows, high, lanes = coarse.shape
    wide = spread_lanes(coarse.reshape(rows * high, lanes), lanes).reshape(rows, high, lanes)
    for h in range(tmp.shape[1]):
        part = wide[..., h * 128 : h * 128 + 128]
        tmp[0:rows, h, pl.ds(0, high, 2), :] = part
        tmp[0:rows, h, pl.ds(1, high, 2), :] = part


def wrap(level, ref, c):
    if level.whole:
        ref[c, 0] = roll(ref[c, level.pairs], level.zlen, 1)
        ref[c, level.pairs + 1] = roll(ref[c, 1], -level.zlen, 1)


def pack(level, get, put):
    s = even_mask(level.high, level.lanes)

    def step(t, _):
        first, second = get(2 * t), get(2 * t + 1)
        put(t, jnp.where(s, first, second), jnp.where(s, second, first))
        return 0

    lax.fori_loop(0, level.pairs, step, 0)


def coefficients(level):
    shape = (level.high, level.lanes)
    s = even_mask(*shape)
    row, lane = iota(shape, 0), iota(shape, 1)
    low_y = row == level.first_y
    top_y = row == level.last_y
    low_z = lane % level.zlen == 0
    top_z = lane % level.zlen == level.zlen - 1
    if level.whole:
        low_x = lane < level.zlen
        top_x = (lane >= (level.gx - 1) * level.zlen) & (lane < level.gx * level.zlen)
    scale = F32(2.0 * 0.25**level.index)
    zero = jnp.zeros(shape, F32)

    def step(t, _):
        at_low = (t == level.first_x).astype(jnp.int32)
        at_top = (t == level.last_x).astype(jnp.int32)
        for c in range(2):
            even = s if c == 0 else ~s
            own, other = level.e[c, t + 1], level.e[1 - c, t + 1]
            outer = jnp.where(even, level.e[1 - c, t], level.e[1 - c, t + 2])
            beyond = jnp.where(even, at_low, at_top) > 0
            if level.whole:
                beyond = beyond & ((even & low_x) | (~even & top_x))

            def weight(n):
                return scale * own * n / (own + n)

            w = [
                weight(other),
                weight(jnp.where(beyond, own, outer)),
                weight(jnp.where(top_y, own, roll(other, -1, 0))),
                weight(jnp.where(low_y, own, roll(other, 1, 0))),
                jnp.where(top_z, zero, weight(roll(other, -1, 1))),
                jnp.where(low_z, zero, weight(roll(other, 1, 1))),
            ]
            total = ((w[0] + w[1]) + (w[2] + w[3])) + (w[4] + w[5])
            inv = 1.0 / total
            level.inv[c, t] = inv
            w[1] = jnp.where(beyond, zero, w[1])
            w[2] = jnp.where(top_y, zero, w[2])
            w[3] = jnp.where(low_y, zero, w[3])
            for k in range(6):
                level.a[c, k, t] = w[k] * inv
        return 0

    lax.fori_loop(0, level.pairs, step, 0)


def updated(level, c, t, s):
    v, a = level.v, level.a
    other = v[1 - c, t + 1]
    even = s if c == 0 else ~s
    outer = jnp.where(even, v[1 - c, t], v[1 - c, t + 2])
    x = level.e[c, t + 1] + a[c, 0, t] * other + a[c, 1, t] * outer
    y = a[c, 2, t] * roll(other, -1, 0) + a[c, 3, t] * roll(other, 1, 0)
    z = a[c, 4, t] * roll(other, -1, 1) + a[c, 5, t] * roll(other, 1, 1)
    return x + (y + z)


def half_sweep(level, c):
    s = even_mask(level.high, level.lanes)

    def step(t, _):
        level.v[c, t + 1] = updated(level, c, t, s)
        return 0

    lax.fori_loop(0, level.pairs, step, 0)
    wrap(level, level.v, c)


def sweeps(level, count):
    def step(_, carry):
        half_sweep(level, 0)
        half_sweep(level, 1)
        return carry

    lax.fori_loop(0, count, step, 0)


def start(level, get):
    def put(t, first, second):
        red = first * level.inv[0, t]
        level.e[0, t + 1] = red
        level.v[0, t + 1] = red
        level.e[1, t + 1] = second * level.inv[1, t]

    pack(level, get, put)
    wrap(level, level.v, 0)
    half_sweep(level, 1)


def residual_sums(level, tmp):
    s = even_mask(level.high, level.lanes)
    lo, rows = level.rim_pairs, level.block_pairs
    ylo, high = level.rim_y, level.block_y

    def step(t, _):
        r = (updated(level, 0, t + lo, s) - level.v[0, t + lo + 1]) / level.inv[0, t + lo]
        put_rows(tmp, t, r[ylo : ylo + high])
        return 0

    lax.fori_loop(0, rows, step, 0)


def coarse_row(level, s, x):
    red, black = level.v[0, x // 2 + 1], level.v[1, x // 2 + 1]
    return jnp.where(s, red, black) if x % 2 == 0 else jnp.where(s, black, red)


def kernel(gx, gy, right_ref, permit_ref, out_ref, refs, lv):
    me_x, me_y = lax.axis_index("gx"), lax.axis_index("gy")
    me = me_x * gy + me_y
    n = gx * gy
    l0, l1, l2, l3, l4 = lv
    send_sem, recv_sem, all_send, all_recv = refs["sems"]

    def inside(dx, dy):
        x, y = me_x + dx, me_y + dy
        return (x >= 0) & (x < gx) & (y >= 0) & (y < gy)

    def cut(d, size, rim, block):
        if d == 0:
            return pl.ds(rim, block), pl.ds(rim, block)
        if d == 1:
            return pl.ds(rim + block - size, size), pl.ds(rim - size, size)
        return pl.ds(rim, size), pl.ds(rim + block, size)

    def copies(kind, src, dst, width, geometry, lead):
        rim_x, block_x, rim_y, block_y = geometry
        out = []
        for k, (dx, dy) in enumerate(DIRS):
            sx, tx = cut(dx, width, rim_x, block_x)
            sy, ty = cut(dy, 8, rim_y, block_y)
            si = (slice(None),) * lead + (sx, sy)
            ti = (slice(None),) * lead + (tx, ty)
            copy = pltpu.make_async_remote_copy(
                src_ref=src.at[si],
                dst_ref=dst.at[ti],
                send_sem=send_sem.at[kind, k],
                recv_sem=recv_sem.at[kind, k],
                device_id=(me_x + dx, me_y + dy),
                device_id_type=MESH,
            )
            out.append((dx, dy, copy))
        return out

    def go(group):
        for dx, dy, copy in group:
            pl.when(inside(dx, dy))(copy.start)

    def arrive(group):
        for dx, dy, copy in group:
            pl.when(inside(-dx, -dy))(copy.wait_recv)

    def sent(group):
        for dx, dy, copy in group:
            pl.when(inside(dx, dy))(copy.wait_send)

    e0, f0, e1, f1 = refs["e0"], refs["f0"], refs["e1"], refs["f1"]
    vh0, vh1 = refs["vh0"], refs["vh1"]
    g0, g1 = (l0.rim_x, l0.block_x, l0.rim_y, l0.block_y), (l1.rim_x, l1.block_x, l1.rim_y, l1.block_y)
    p0, p1 = (l0.rim_pairs + 1, l0.block_pairs) + g0[2:], (l1.rim_pairs + 1, l1.block_pairs) + g1[2:]
    deep = 2 * SMOOTH
    send_e0 = copies(0, e0, e0, deep + 1, g0, 0)
    send_f0 = copies(1, f0, f0, deep, g0, 0)
    send_e1 = copies(2, e1, e1, deep + 2, g1, 0)
    send_f1 = copies(3, f1, f1, deep + 1, g1, 0)
    send_v0 = copies(4, l0.v, vh0, deep // 2, p0, 1)
    send_v1 = copies(5, l1.v, vh1, deep // 2 + 1, p1, 1)

    for ref, value in ((e0, 1.0), (f0, 0.0), (e1, 1.0), (f1, 0.0)):
        ref[...] = jnp.full(ref.shape, value, F32)
    vh0[...] = jnp.zeros(vh0.shape, F32)
    vh1[...] = jnp.zeros(vh1.shape, F32)
    x0, y0 = pl.ds(l0.rim_x, l0.block_x), pl.ds(l0.rim_y, l0.block_y)
    e0[x0, y0, :] = permit_ref[...]
    f0[x0, y0, :] = right_ref[...]

    barrier = pltpu.get_barrier_semaphore()

    def device(d):
        t = lax.rem(me + d, n)
        return (lax.div(t, gy), lax.rem(t, gy))

    def greet(d, _):
        pl.semaphore_signal(barrier, inc=1, device_id=device(d), device_id_type=MESH)
        return 0

    lax.fori_loop(1, n, greet, 0)
    pl.semaphore_wait(barrier, n - 1)

    go(send_e0)
    go(send_f0)

    for level in (l0, l1, l2, l3, l4):
        level.v[...] = jnp.zeros(level.v.shape, F32)
    l0.e[...] = jnp.ones(l0.e.shape, F32)
    l1.e[...] = jnp.ones(l1.e.shape, F32)

    tmp = refs["tmp"]
    lanes = l0.lanes

    def narrow(values, used, other):
        lane = iota(values.shape, len(values.shape) - 1)
        return jnp.where(lane < used, values, F32(other))

    put_rows(
        tmp,
        pl.ds(0, l1.block_x),
        permit_ref[...].reshape(l1.block_x, 2, l0.block_y, lanes).sum(axis=1),
    )
    own_e1 = narrow(restrict(tmp, l1.block_x, l0.block_y), l1.zlen, 1.0)
    e1[pl.ds(l1.rim_x, l1.block_x), pl.ds(l1.rim_y, l1.block_y), :] = own_e1
    go(send_e1)

    block2, z2 = l2.block_x, l2.zlen
    per = 128 // z2
    groups = block2 // per

    def gather_start(kind, rows):
        stage, packed = refs["stage"].at[kind], refs["packed"].at[kind]
        group = iota((8, 128), 1) // z2
        for g in range(groups):
            value = rows[g * per]
            for k in range(1, per):
                value = jnp.where(group == k, roll(rows[g * per + k], k * z2, 1), value)
            packed[g] = value
            stage[me, g] = value

        def step(d, _):
            pltpu.make_async_remote_copy(
                src_ref=packed,
                dst_ref=stage.at[me],
                send_sem=all_send.at[kind],
                recv_sem=all_recv.at[kind],
                device_id=device(d),
                device_id_type=MESH,
            ).start()
            return 0

        lax.fori_loop(1, n, step, 0)

    def gather_wait(kind, full):
        stage = refs["stage"].at[kind]
        others = stage.at[pl.ds(0, n - 1)]
        pltpu.make_async_copy(others, others, all_recv.at[kind]).wait()
        group = iota((8, 128), 1) // z2

        def step(q, _):
            for x in range(block2):
                tiles = []
                for h in range(full.shape[-1] // 128):
                    value = None
                    for k in range(per):
                        p = h * per + k
                        if p >= gx:
                            break
                        part = roll(stage[p * gy + q, x // per], (k - x % per) * z2, 1)
                        value = part if k == 0 else jnp.where(group == k, part, value)
                    tiles.append(value)
                row = tiles[0] if len(tiles) == 1 else jnp.concatenate(tiles, axis=1)
                full[x, pl.ds(pl.multiple_of(q * 8 + 8, 8), 8), :] = row
            return 0

        lax.fori_loop(0, gy, step, 0)

    def gather_end(kind):
        others = refs["stage"].at[kind, pl.ds(0, n - 1)]
        pltpu.make_async_copy(others, others, all_send.at[kind]).wait()

    put_rows(tmp, pl.ds(0, block2), own_e1.reshape(block2, 2, l1.block_y, lanes).sum(axis=1))
    gather_start(0, restrict(tmp, block2, l1.block_y))

    def put_e(level):
        def put(t, first, second):
            level.e[0, t + 1] = first
            level.e[1, t + 1] = second

        return put

    arrive(send_e0)
    pack(l0, lambda x: e0[x], put_e(l0))
    coefficients(l0)
    arrive(send_f0)
    start(l0, lambda x: f0[x])
    sweeps(l0, SMOOTH - 1)
    go(send_v0)
    residual_sums(l0, tmp)
    f1[pl.ds(l1.rim_x, l1.block_x), pl.ds(l1.rim_y, l1.block_y), :] = restrict(
        tmp, l1.block_x, l0.block_y
    )
    go(send_f1)

    arrive(send_e1)
    pack(l1, lambda x: e1[x], put_e(l1))
    coefficients(l1)
    arrive(send_f1)
    start(l1, lambda x: f1[x])
    sweeps(l1, SMOOTH - 1)
    go(send_v1)
    residual_sums(l1, tmp)
    gather_start(1, restrict(tmp, block2, l1.block_y))

    full, big = refs["full"], refs["big"]
    full[...] = jnp.zeros(full.shape, F32)
    gather_wait(0, full)
    pack(l2, lambda x: full[x, 8 : 8 + l2.high], put_e(l2))
    for fine, coarse in ((l2, l3), (l3, l4)):
        for c in range(2):
            wrap(fine, fine.e, c)
        coefficients(fine)
        for t in range(fine.pairs):
            put_rows(big, t, fine.e[0, t + 1] + fine.e[1, t + 1])
        rows = narrow(restrict(big, fine.pairs, fine.high), gx * coarse.zlen, 1.0)
        coarse.full[...] = rows
        pack(coarse, lambda x: coarse.full[x], put_e(coarse))
    for c in range(2):
        wrap(l4, l4.e, c)
    coefficients(l4)

    gather_wait(1, full)
    start(l2, lambda x: full[x, 8 : 8 + l2.high])
    sweeps(l2, SMOOTH - 1)
    for fine, coarse in ((l2, l3), (l3, l4)):
        residual_sums(fine, big)
        coarse.full[...] = restrict(big, fine.pairs, fine.high)
        start(coarse, lambda x: coarse.full[x])
        sweeps(coarse, SMOOTH - 1 if coarse is l3 else COARSE_SWEEPS - 1)

    def correct(fine, coarse):
        s = even_mask(coarse.high, coarse.lanes)
        spread(big, jnp.stack([coarse_row(coarse, s, t) for t in range(fine.pairs)]))
        for c in range(2):
            for t in range(fine.pairs):
                fine.v[c, t + 1] = fine.v[c, t + 1] + get_row(big, t, fine.high)
            wrap(fine, fine.v, c)
        sweeps(fine, SMOOTH)

    correct(l3, l4)
    correct(l2, l3)

    def joined(level, halo, c, t):
        lo, hi = level.rim_y, level.rim_y + level.block_y
        return jnp.concatenate(
            [halo[c, t, 0:lo], level.v[c, t, lo:hi], halo[c, t, hi : level.high]], axis=0
        )

    def add(level, halo):
        lo, hi = level.rim_pairs, level.rim_pairs + level.block_pairs
        for c in range(2):
            for t in list(range(lo)) + list(range(hi, level.pairs)):
                level.v[c, t + 1] = halo[c, t + 1] + get_row(tmp, t, level.high)

            def step(t, _):
                level.v[c, t + 1] = joined(level, halo, c, t + 1) + get_row(tmp, t, level.high)
                return 0

            lax.fori_loop(lo, hi, step, 0)

    s2 = even_mask(l2.high, l2.lanes)
    for x in range(block2):
        full[x, 8 : 8 + l2.high, :] = coarse_row(l2, s2, x)
    rows = []
    high = l1.high // 2
    skip = 8 - l1.rim_y // 2
    for t in range(l1.pairs):
        x = t - l1.rim_pairs
        p = lax.rem(me_x + x // block2 + gx, gx)
        value = full[x % block2, pl.ds(pl.multiple_of(me_y * 8, 8), 24), :]
        value = pltpu.roll(value, lax.rem(l2.lanes - p * z2, l2.lanes), 1)
        rows.append(value[skip : skip + high, 0:128])
    arrive(send_v1)
    sent(send_v1)
    spread(tmp, jnp.stack(rows))
    add(l1, vh1)
    sweeps(l1, SMOOTH)

    s1 = even_mask(l1.high, l1.lanes)
    first = l1.rim_x - l0.rim_pairs
    low = l1.rim_y - l0.rim_y // 2
    rows = [coarse_row(l1, s1, first + t)[low : low + l0.high // 2] for t in range(l0.pairs)]
    arrive(send_v0)
    sent(send_v0)
    spread(tmp, jnp.stack(rows))
    add(l0, vh0)
    sweeps(l0, SMOOTH)

    s0 = even_mask(l0.high, l0.lanes)

    def last(t, _):
        red, black = l0.v[0, t + l0.rim_pairs + 1], l0.v[1, t + l0.rim_pairs + 1]
        lo, hi = l0.rim_y, l0.rim_y + l0.block_y
        out_ref[2 * t] = jnp.where(s0, red, black)[lo:hi]
        out_ref[2 * t + 1] = jnp.where(s0, black, red)[lo:hi]
        return 0

    lax.fori_loop(0, l0.block_pairs, last, 0)
    for group in (send_e0, send_f0, send_e1, send_f1):
        sent(group)
    for kind in range(2):
        gather_end(kind)


def per_device(gx, gy, right_side, permittivity):
    bx, by, nz = right_side.shape
    n = gx * gy
    wide = -(-gx * (nz // 4) // 128) * 128
    scratch, names = [], []

    def buffer(owner, name, *shape):
        scratch.append(pltpu.VMEM(shape, F32))
        names.append((owner, name))

    refs = {}
    levels = []
    for index in range(LEVELS):
        level = Level()
        level.index, level.gx = index, gx
        level.zlen = nz >> index
        level.whole = index >= 2
        level.block_x = bx >> index
        if level.whole:
            level.rim_x = level.rim_y = level.rim_pairs = 0
            level.pairs = level.block_pairs = level.block_x // 2
            level.high = level.block_y = (by >> index) * gy
            level.lanes = wide
        else:
            level.rim_x, level.rim_y = 6, 8
            level.block_y = by >> index
            level.rim_pairs, level.block_pairs = level.rim_x // 2, level.block_x // 2
            level.pairs = level.block_pairs + 2 * level.rim_pairs
            level.high = level.block_y + 2 * level.rim_y
            level.lanes = nz
        size = (level.high, level.lanes)
        buffer(level, "e", 2, level.pairs + 2, *size)
        buffer(level, "v", 2, level.pairs + 2, *size)
        buffer(level, "inv", 2, level.pairs, *size)
        buffer(level, "a", 2, 6, level.pairs, *size)
        if index < 2:
            buffer(None, f"e{index}", 2 * level.pairs, *size)
            buffer(None, f"f{index}", 2 * level.pairs, *size)
            buffer(None, f"vh{index}", 2, level.pairs + 2, *size)
        if index == 2:
            buffer(None, "big", level.pairs, level.lanes // 128, level.high, 128)
            buffer(None, "full", level.block_x, level.high + 16, level.lanes)
        if index > 2:
            buffer(level, "full", level.block_x, *size)
        levels.append(level)
    l0 = levels[0]
    buffer(None, "tmp", l0.pairs, 1, l0.high, l0.lanes)
    groups = levels[2].block_x // (128 // levels[2].zlen)
    buffer(None, "stage", 2, n, groups, 8, 128)
    buffer(None, "packed", 2, groups, 8, 128)
    sems = [
        pltpu.SemaphoreType.DMA((6, 8)),
        pltpu.SemaphoreType.DMA((6, 8)),
        pltpu.SemaphoreType.DMA((2,)),
        pltpu.SemaphoreType.DMA((2,)),
    ]

    def body(right_ref, permit_ref, out_ref, *buffers):
        me_x, me_y = lax.axis_index("gx"), lax.axis_index("gy")
        for (owner, name), ref in zip(names, buffers):
            if owner is None:
                refs[name] = ref
            else:
                setattr(owner, name, ref)
        refs["sems"] = buffers[len(names) :]
        for level in levels:
            if level.whole:
                level.first_x, level.last_x = 0, level.pairs - 1
                level.first_y, level.last_y = 0, level.high - 1
            else:
                level.first_x = level.rim_pairs - me_x * level.block_pairs
                level.last_x = level.first_x + gx * level.block_pairs - 1
                level.first_y = level.rim_y - me_y * level.block_y
                level.last_y = level.first_y + gy * level.block_y - 1
        kernel(gx, gy, right_ref, permit_ref, out_ref, refs, levels)

    return pl.pallas_call(
        body,
        out_shape=jax.ShapeDtypeStruct(right_side.shape, F32),
        in_specs=[pl.BlockSpec(memory_space=pltpu.VMEM)] * 2,
        out_specs=pl.BlockSpec(memory_space=pltpu.VMEM),
        scratch_shapes=scratch + sems,
        compiler_params=pltpu.CompilerParams(
            collective_id=0, has_side_effects=True, vmem_limit_bytes=60 * 2**20
        ),
    )(right_side, permittivity)


def solution(mesh):
    gx, gy = mesh.shape["gx"], mesh.shape["gy"]
    placed = (P("gx", "gy", None), P("gx", "gy", None))
    return jax.shard_map(
        functools.partial(per_device, gx, gy),
        mesh=mesh,
        in_specs=placed,
        out_specs=P("gx", "gy", None),
        check_vma=False,
    )
```

```python
import functools

import jax
import jax.numpy as jnp
from jax import lax
from jax.experimental import pallas as pl
from jax.experimental.pallas import tpu as pltpu
from jax.sharding import PartitionSpec as P

LEVELS = 5
SMOOTH = 2
COARSE_SWEEPS = 12
MESH = pl.DeviceIdType.MESH
F32 = jnp.float32


DIRS = [(dx, dy) for dx in (-1, 0, 1) for dy in (-1, 0, 1) if (dx, dy) != (0, 0)]
DIRS.sort(key=lambda d: (d[0] == 0, d[1] != 0))


class Level:
    pass


def iota(shape, dim):
    return lax.broadcasted_iota(jnp.int32, shape, dim)


def even_mask(rows, lanes):
    return (iota((rows, lanes), 0) + iota((rows, lanes), 1)) % 2 == 0


def roll(x, shift, axis):
    return pltpu.roll(x, shift % x.shape[axis], axis)


def sum_lanes(x, lanes):
    pick = jnp.where(iota((lanes, lanes), 0) // 2 == iota((lanes, lanes), 1), F32(0.125), F32(0.0))
    return jnp.dot(x, pick, precision=lax.Precision.HIGHEST, preferred_element_type=F32)


def spread_lanes(x, lanes):
    pick = jnp.where(iota((lanes, lanes), 0) == iota((lanes, lanes), 1) // 2, F32(1.0), F32(0.0))
    return jnp.dot(x, pick, precision=lax.Precision.HIGHEST, preferred_element_type=F32)


def put_rows(tmp, t, values):
    for h in range(tmp.shape[1]):
        tmp[t, h, 0 : values.shape[-2], :] = values[..., h * 128 : h * 128 + 128]


def get_row(tmp, t, high):
    tiles = [tmp[t, h, 0:high, :] for h in range(tmp.shape[1])]
    return tiles[0] if len(tiles) == 1 else jnp.concatenate(tiles, axis=-1)


def get_strided(tmp, rows, count, first):
    tiles = [tmp[0:rows, h, pl.ds(first, count, 2), :] for h in range(tmp.shape[1])]
    return tiles[0] if len(tiles) == 1 else jnp.concatenate(tiles, axis=-1)


def restrict(tmp, rows, high):
    lanes = tmp.shape[1] * 128
    both = get_strided(tmp, rows, high // 2, 0) + get_strided(tmp, rows, high // 2, 1)
    flat = both.reshape(rows * (high // 2), lanes)
    return sum_lanes(flat, lanes).reshape(rows, high // 2, lanes)


def spread(tmp, coarse):
    rows, high, lanes = coarse.shape
    wide = spread_lanes(coarse.reshape(rows * high, lanes), lanes).reshape(rows, high, lanes)
    for h in range(tmp.shape[1]):
        part = wide[..., h * 128 : h * 128 + 128]
        tmp[0:rows, h, pl.ds(0, high, 2), :] = part
        tmp[0:rows, h, pl.ds(1, high, 2), :] = part


def wrap(level, ref):
    if level.whole:
        ref[0] = roll(ref[level.pairs], level.zlen, 1)
        ref[level.pairs + 1] = roll(ref[1], -level.zlen, 1)


def inverse(x):
    y = pl.reciprocal(x, approx=True)
    y = y * (2.0 - x * y)
    return y * (2.0 - x * y)


def loop(level, lo, hi, body):
    size = min(hi - lo, max(1, 32 * 1024 // (level.high * level.lanes)))
    if size < 1:
        return
    full = (hi - lo) // size

    def step(i, _):
        for k in range(size):
            body(lo + i * size + k)
        return 0

    if full > 1:
        lax.fori_loop(0, full, step, 0)
    else:
        step(0, 0)
    for t in range(lo + full * size, hi):
        body(t)


def reach(level, cells):
    if level.whole:
        return 0, level.pairs
    more = (cells + 1) // 2
    return level.rim_pairs - more, level.rim_pairs + level.block_pairs + more


def pack(level, get, put, lo, hi):
    s = even_mask(level.high, level.lanes)

    def step(t):
        first, second = get(2 * t), get(2 * t + 1)
        put(t, jnp.where(s, first, second), jnp.where(s, second, first))

    loop(level, lo, hi, step)


def put_e(level):
    def put(t, first, second):
        level.e[0][t + 1] = first
        level.e[1][t + 1] = second

    return put


class Ends:
    def __init__(self, level):
        shape = (level.high, level.lanes)
        row, lane = iota(shape, 0), iota(shape, 1)
        self.level = level
        self.s = even_mask(*shape)
        self.low_y, self.top_y = row == level.first_y, row == level.last_y
        self.low_z = lane % level.zlen == 0
        self.top_z = lane % level.zlen == level.zlen - 1
        if level.whole:
            self.low_x = lane < level.zlen
            self.top_x = (lane >= (level.gx - 1) * level.zlen) & (lane < level.gx * level.zlen)

    def beyond(self, c, t):
        level = self.level
        even = self.s if c == 0 else ~self.s
        at_low = jnp.asarray(t == level.first_x).astype(jnp.int32)
        at_top = jnp.asarray(t == level.last_x).astype(jnp.int32)
        out = jnp.where(even, at_low, at_top) > 0
        if level.whole:
            out = out & ((even & self.low_x) | (~even & self.top_x))
        return out


def finish(level, ends, c, t, w, beyond):
    total = ((w[0] + w[1]) + (w[2] + w[3])) + (w[4] + w[5])
    inv = inverse(total)
    level.inv[c, t] = inv
    w = list(w)
    w[1] = jnp.where(beyond, 0.0, w[1])
    w[2] = jnp.where(ends.top_y, 0.0, w[2])
    w[3] = jnp.where(ends.low_y, 0.0, w[3])
    for k in range(6):
        level.a[c, k, t] = w[k] * inv


def red_weights(level, ends, lo, hi):
    scale = F32(2.0 * 0.25**level.index)
    end_scale = F32(0.25**level.index)
    s = ends.s

    def step(t):
        own, other = level.e[0][t + 1], level.e[1][t + 1]
        outer = jnp.where(s, level.e[1][t], level.e[1][t + 2])
        scaled, end = scale * own, end_scale * own
        beyond = ends.beyond(0, t)

        def weight(n):
            return scaled * n * inverse(own + n)

        w = [
            weight(other),
            weight(outer),
            weight(roll(other, -1, 0)),
            weight(roll(other, 1, 0)),
            jnp.where(ends.top_z, 0.0, weight(roll(other, -1, 1))),
            jnp.where(ends.low_z, 0.0, weight(roll(other, 1, 1))),
        ]
        level.v[0][t + 1] = w[1]
        level.a[1, 0, t] = w[0]
        level.a[1, 2, t] = roll(w[3], -1, 0)
        level.a[1, 3, t] = roll(w[2], 1, 0)
        level.a[1, 4, t] = roll(w[5], -1, 1)
        level.a[1, 5, t] = roll(w[4], 1, 1)
        w[1] = jnp.where(beyond, end, w[1])
        w[2] = jnp.where(ends.top_y, end, w[2])
        w[3] = jnp.where(ends.low_y, end, w[3])
        finish(level, ends, 0, t, w, beyond)

    lax.fori_loop(lo, hi, lambda t, c: (step(t), c)[1], 0)


def black_weights(level, ends, lo, hi):
    end_scale = F32(0.25**level.index)

    def step(t):
        end = end_scale * level.e[1][t + 1]
        beyond = ends.beyond(1, t)
        w = [level.a[1, k, t] for k in (0, 0, 2, 3, 4, 5)]
        w[1] = jnp.where(ends.s, level.v[0][t + 2], level.v[0][t])
        w[1] = jnp.where(beyond, end, w[1])
        w[2] = jnp.where(ends.top_y, end, w[2])
        w[3] = jnp.where(ends.low_y, end, w[3])
        finish(level, ends, 1, t, w, beyond)

    lax.fori_loop(lo, hi, lambda t, c: (step(t), c)[1], 0)


def coefficients(level, cells):
    ends = Ends(level)
    lo, hi = reach(level, cells)
    more = 0 if level.whole else 1
    red_weights(level, ends, lo - more, hi + more)
    wrap(level, level.v[0])
    black_weights(level, ends, lo, hi)


def updated(level, c, t, s):
    v, a = level.v[1 - c], level.a
    other = v[t + 1]
    even = s if c == 0 else ~s
    outer = jnp.where(even, v[t], v[t + 2])
    x = level.e[c][t + 1] + a[c, 0, t] * other + a[c, 1, t] * outer
    y = a[c, 2, t] * roll(other, -1, 0) + a[c, 3, t] * roll(other, 1, 0)
    z = a[c, 4, t] * roll(other, -1, 1) + a[c, 5, t] * roll(other, 1, 1)
    return x + (y + z)


def half_sweep(level, c, cells):
    s = even_mask(level.high, level.lanes)

    def step(t):
        level.v[c][t + 1] = updated(level, c, t, s)

    loop(level, *reach(level, cells), step)
    wrap(level, level.v[c])


def sweeps(level, count, cells):
    for k in range(2 * count):
        half_sweep(level, k % 2, cells + 2 * count - 1 - k)


def start(level, get, cells, keep):
    def put(t, first, second):
        red = first * level.inv[0, t]
        level.e[0][t + 1] = red
        level.v[0][t + 1] = red
        level.e[1][t + 1] = second * level.inv[1, t]

    pack(level, get, put, *reach(level, keep))
    wrap(level, level.v[0])
    if cells is not None:
        half_sweep(level, 1, cells)


def solve_small(level, count):
    s = even_mask(level.high, level.lanes)
    a = [[level.a[c, k, 0] for k in range(6)] for c in range(2)]
    f = [level.e[c][1] for c in range(2)]

    def half(c, other):
        even = s if c == 0 else ~s
        outer = jnp.where(even, roll(other, level.zlen, 1), roll(other, -level.zlen, 1))
        x = f[c] + a[c][0] * other + a[c][1] * outer
        y = a[c][2] * roll(other, -1, 0) + a[c][3] * roll(other, 1, 0)
        z = a[c][4] * roll(other, -1, 1) + a[c][5] * roll(other, 1, 1)
        return x + (y + z)

    def step(_, v):
        red = half(0, v[1])
        return red, half(1, red)

    first = f[0]
    v = lax.fori_loop(0, count - 1, step, (first, half(1, first)))
    for c in range(2):
        level.v[c][1] = v[c]


def residual_sums(level, tmp):
    s = even_mask(level.high, level.lanes)
    lo, hi = reach(level, 0)
    ylo, high = level.rim_y, level.block_y

    def step(t):
        r = (updated(level, 0, t, s) - level.v[0][t + 1]) * inverse(level.inv[0, t])
        put_rows(tmp, t - lo, r[ylo : ylo + high])

    loop(level, lo, hi, step)


def coarse_row(level, s, x):
    red, black = level.v[0][x // 2 + 1], level.v[1][x // 2 + 1]
    return jnp.where(s, red, black) if x % 2 == 0 else jnp.where(s, black, red)


def kernel(gx, gy, right_ref, permit_ref, out_ref, refs, lv):
    me_x, me_y = lax.axis_index("gx"), lax.axis_index("gy")
    me = me_x * gy + me_y
    n = gx * gy
    l0, l1, l2, l3, l4 = lv
    send_sem, recv_sem, all_send, all_recv = refs["sems"]

    def inside(dx, dy):
        x, y = me_x + dx, me_y + dy
        return (x >= 0) & (x < gx) & (y >= 0) & (y < gy)

    def cut(d, size, rim, block):
        if d == 0:
            return pl.ds(rim, block), pl.ds(rim, block)
        if d == 1:
            return pl.ds(rim + block - size, size), pl.ds(rim - size, size)
        return pl.ds(rim, size), pl.ds(rim + block, size)

    def copies(kind, src, dst, width, geometry):
        rim_x, block_x, rim_y, block_y = geometry
        out = []
        for k, (dx, dy) in enumerate(DIRS):
            sx, tx = cut(dx, width, rim_x, block_x)
            sy, ty = cut(dy, 8, rim_y, block_y)
            copy = pltpu.make_async_remote_copy(
                src_ref=src.at[sx, sy],
                dst_ref=dst.at[tx, ty],
                send_sem=send_sem.at[kind, k],
                recv_sem=recv_sem.at[kind, k],
                device_id=(me_x + dx, me_y + dy),
                device_id_type=MESH,
            )
            out.append((dx, dy, copy))
        return out

    def go(group):
        for dx, dy, copy in group:
            pl.when(inside(dx, dy))(copy.start)

    def arrive(group):
        for dx, dy, copy in group:
            pl.when(inside(-dx, -dy))(copy.wait_recv)

    def sent(group):
        for dx, dy, copy in group:
            pl.when(inside(dx, dy))(copy.wait_send)

    e0, f0, e1, f1 = refs["e0"], refs["f0"], refs["e1"], refs["f1"]
    vh0, vh1 = refs["vh0"], refs["vh1"]
    g0, g1 = (l0.rim_x, l0.block_x, l0.rim_y, l0.block_y), (l1.rim_x, l1.block_x, l1.rim_y, l1.block_y)
    p0, p1 = (l0.rim_pairs + 1, l0.block_pairs) + g0[2:], (l1.rim_pairs + 1, l1.block_pairs) + g1[2:]
    deep = 2 * SMOOTH
    send_e0 = copies(0, e0, e0, deep + 1, g0)
    send_f0 = copies(1, f0, f0, deep, g0)
    send_e1 = copies(2, e1, e1, deep + 2, g1)
    send_f1 = copies(3, f1, f1, deep + 1, g1)
    send_v0, send_v1 = [], []
    for c in range(2):
        send_v0 += copies(4 + c, l0.v[c], vh0.at[c], deep // 2, p0)
        send_v1 += copies(6 + c, l1.v[c], vh1.at[c], deep // 2 + 1, p1)

    def fill(ref, lead, value, geometry):
        rim_x, block_x, rim_y, block_y = geometry
        rows, high, width = ref.shape[-3:]
        top_x, top_y = rim_x + block_x, rim_y + block_y
        for xs, ys in (
            ((0, rim_x), (0, high)),
            ((top_x, rows), (0, high)),
            ((rim_x, top_x), (0, rim_y)),
            ((rim_x, top_x), (top_y, high)),
        ):
            part = jnp.full((xs[1] - xs[0], ys[1] - ys[0], width), value, F32)
            ref[lead + (slice(*xs), slice(*ys))] = part

    fill(e0, (), 1.0, g0)
    fill(f0, (), 0.0, g0)
    fill(e1, (), 1.0, g1)
    fill(f1, (), 0.0, g1)
    for c in range(2):
        fill(vh0, (c,), 0.0, p0)
        fill(vh1, (c,), 0.0, p1)
    x0, y0 = pl.ds(l0.rim_x, l0.block_x), pl.ds(l0.rim_y, l0.block_y)
    e0[x0, y0, :] = permit_ref[...]
    f0[x0, y0, :] = right_ref[...]

    barrier = pltpu.get_barrier_semaphore()

    def device(d):
        t = lax.rem(me + d, n)
        return (lax.div(t, gy), lax.rem(t, gy))

    def greet(d, _):
        pl.semaphore_signal(barrier, inc=1, device_id=device(d), device_id_type=MESH)
        return 0

    lax.fori_loop(1, n, greet, 0)
    for level in (l0, l1):
        for c in range(2):
            for t in list(range(3)) + list(range(level.pairs - 1, level.pairs + 2)):
                level.v[c][t] = jnp.zeros((level.high, level.lanes), F32)
            for t in (0, level.pairs + 1):
                level.e[c][t] = jnp.ones((level.high, level.lanes), F32)
    pl.semaphore_wait(barrier, n - 1)

    go(send_e0)
    go(send_f0)

    tmp = refs["tmp"]
    lanes = l0.lanes

    def narrow(values, used, other):
        lane = iota(values.shape, len(values.shape) - 1)
        return jnp.where(lane < used, values, F32(other))

    put_rows(
        tmp,
        pl.ds(0, l1.block_x),
        permit_ref[...].reshape(l1.block_x, 2, l0.block_y, lanes).sum(axis=1),
    )
    own_e1 = narrow(restrict(tmp, l1.block_x, l0.block_y), l1.zlen, 1.0)
    e1[pl.ds(l1.rim_x, l1.block_x), pl.ds(l1.rim_y, l1.block_y), :] = own_e1
    go(send_e1)

    block2, z2 = l2.block_x, l2.zlen
    per = 128 // z2
    groups = block2 // per

    def gather_start(kind, rows):
        stage, packed = refs["stage"].at[kind], refs["packed"].at[kind]
        group = iota((8, 128), 1) // z2
        for g in range(groups):
            value = rows[g * per]
            for k in range(1, per):
                value = jnp.where(group == k, roll(rows[g * per + k], k * z2, 1), value)
            packed[g] = value
            stage[me, g] = value

        def step(d, _):
            pltpu.make_async_remote_copy(
                src_ref=packed,
                dst_ref=stage.at[me],
                send_sem=all_send.at[kind],
                recv_sem=all_recv.at[kind],
                device_id=device(d),
                device_id_type=MESH,
            ).start()
            return 0

        lax.fori_loop(1, n, step, 0)

    def gather_wait(kind, full):
        stage = refs["stage"].at[kind]
        others = stage.at[pl.ds(0, n - 1)]
        pltpu.make_async_copy(others, others, all_recv.at[kind]).wait()
        group = iota((8, 128), 1) // z2

        def step(q, _):
            for x in range(block2):
                tiles = []
                for h in range(full.shape[-1] // 128):
                    value = None
                    for k in range(per):
                        p = h * per + k
                        if p >= gx:
                            break
                        part = roll(stage[p * gy + q, x // per], (k - x % per) * z2, 1)
                        value = part if k == 0 else jnp.where(group == k, part, value)
                    tiles.append(value)
                row = tiles[0] if len(tiles) == 1 else jnp.concatenate(tiles, axis=1)
                full[x, pl.ds(pl.multiple_of(q * 8 + 8, 8), 8), :] = row
            return 0

        lax.fori_loop(0, gy, step, 0)

    def gather_end(kind):
        others = refs["stage"].at[kind, pl.ds(0, n - 1)]
        pltpu.make_async_copy(others, others, all_send.at[kind]).wait()

    put_rows(tmp, pl.ds(0, block2), own_e1.reshape(block2, 2, l1.block_y, lanes).sum(axis=1))
    gather_start(0, restrict(tmp, block2, l1.block_y))

    arrive([item for item in send_e0 if item[0] == 0])
    lo, hi = reach(l0, 0)
    ends = Ends(l0)
    pack(l0, lambda x: e0[x], put_e(l0), lo, hi)
    red_weights(l0, ends, lo + 1, hi - 1)
    black_weights(l0, ends, lo + 2, hi - 2)
    arrive([item for item in send_e0 if item[0] != 0])
    far_lo, far_hi = reach(l0, deep)
    pack(l0, lambda x: e0[x], put_e(l0), 0, lo)
    pack(l0, lambda x: e0[x], put_e(l0), hi, l0.pairs)
    red_weights(l0, ends, far_lo - 1, lo + 1)
    red_weights(l0, ends, hi - 1, far_hi + 1)
    black_weights(l0, ends, far_lo, lo + 2)
    black_weights(l0, ends, hi - 2, far_hi)
    arrive(send_f0)
    start(l0, lambda x: f0[x], deep - 1, deep)
    sweeps(l0, SMOOTH - 1, 1)
    go(send_v0)
    residual_sums(l0, tmp)
    f1[pl.ds(l1.rim_x, l1.block_x), pl.ds(l1.rim_y, l1.block_y), :] = restrict(
        tmp, l1.block_x, l0.block_y
    )
    go(send_f1)

    arrive(send_e1)
    pack(l1, lambda x: e1[x], put_e(l1), 0, l1.pairs)
    coefficients(l1, deep)
    arrive(send_f1)
    start(l1, lambda x: f1[x], deep - 1, deep + 1)
    sweeps(l1, SMOOTH - 1, 1)
    go(send_v1)
    residual_sums(l1, tmp)
    gather_start(1, restrict(tmp, block2, l1.block_y))

    full, big = refs["full"], refs["big"]
    full[...] = jnp.zeros(full.shape, F32)
    gather_wait(0, full)
    pack(l2, lambda x: full[x, 8 : 8 + l2.high], put_e(l2), 0, l2.pairs)
    for fine, coarse in ((l2, l3), (l3, l4)):
        for c in range(2):
            wrap(fine, fine.e[c])
        coefficients(fine, 0)
        for t in range(fine.pairs):
            put_rows(big, t, fine.e[0][t + 1] + fine.e[1][t + 1])
        rows = narrow(restrict(big, fine.pairs, fine.high), gx * coarse.zlen, 1.0)
        coarse.full[...] = rows
        pack(coarse, lambda x: coarse.full[x], put_e(coarse), 0, coarse.pairs)
    for c in range(2):
        wrap(l4, l4.e[c])
    coefficients(l4, 0)

    gather_wait(1, full)
    start(l2, lambda x: full[x, 8 : 8 + l2.high], 0, 0)
    sweeps(l2, SMOOTH - 1, 0)
    for fine, coarse in ((l2, l3), (l3, l4)):
        residual_sums(fine, big)
        coarse.full[...] = restrict(big, fine.pairs, fine.high)
        small = coarse is l4 and coarse.pairs == 1
        start(coarse, lambda x: coarse.full[x], None if small else 0, 0)
        if small:
            solve_small(coarse, COARSE_SWEEPS)
        else:
            sweeps(coarse, SMOOTH - 1 if coarse is l3 else COARSE_SWEEPS - 1, 0)

    def correct(fine, coarse):
        s = even_mask(coarse.high, coarse.lanes)
        spread(big, jnp.stack([coarse_row(coarse, s, t) for t in range(fine.pairs)]))
        for c in range(2):
            for t in range(fine.pairs):
                fine.v[c][t + 1] = fine.v[c][t + 1] + get_row(big, t, fine.high)
            wrap(fine, fine.v[c])
        sweeps(fine, SMOOTH, 0)

    correct(l3, l4)
    correct(l2, l3)

    def add(level, halo, far_lo, far_hi):
        lo, hi = reach(level, 0)
        ylo, yhi = level.rim_y, level.rim_y + level.block_y
        for c in range(2):
            for t in list(range(far_lo, lo)) + list(range(hi, far_hi)):
                level.v[c][t + 1] = halo[c, t + 1] + get_row(tmp, t - far_lo, level.high)

            def step(t):
                row = jnp.concatenate(
                    [
                        halo[c, t + 1, 0:ylo],
                        level.v[c][t + 1, ylo:yhi],
                        halo[c, t + 1, yhi : level.high],
                    ],
                    axis=0,
                )
                level.v[c][t + 1] = row + get_row(tmp, t - far_lo, level.high)

            loop(level, lo, hi, step)

    s2 = even_mask(l2.high, l2.lanes)
    for x in range(block2):
        full[x, 8 : 8 + l2.high, :] = coarse_row(l2, s2, x)
    rows = []
    high = l1.high // 2
    skip = 8 - l1.rim_y // 2
    for t in range(l1.pairs):
        x = t - l1.rim_pairs
        p = lax.rem(me_x + x // block2 + gx, gx)
        value = full[x % block2, pl.ds(pl.multiple_of(me_y * 8, 8), 24), :]
        value = pltpu.roll(value, lax.rem(l2.lanes - p * z2, l2.lanes), 1)
        rows.append(value[skip : skip + high, 0:128])
    arrive(send_v1)
    sent(send_v1)
    spread(tmp, jnp.stack(rows))
    add(l1, vh1, 0, l1.pairs)
    sweeps(l1, SMOOTH, 2)

    s1 = even_mask(l1.high, l1.lanes)
    first = l1.rim_x - l0.rim_pairs
    low = l1.rim_y - l0.rim_y // 2
    far_lo, far_hi = reach(l0, deep)
    rows = [coarse_row(l1, s1, first + t)[low : low + l0.high // 2] for t in range(far_lo, far_hi)]
    arrive(send_v0)
    sent(send_v0)
    spread(tmp, jnp.stack(rows))
    add(l0, vh0, far_lo, far_hi)
    sweeps(l0, SMOOTH, 0)

    s0 = even_mask(l0.high, l0.lanes)

    def last(t):
        red, black = l0.v[0][t + l0.rim_pairs + 1], l0.v[1][t + l0.rim_pairs + 1]
        lo, hi = l0.rim_y, l0.rim_y + l0.block_y
        out_ref[2 * t] = jnp.where(s0, red, black)[lo:hi]
        out_ref[2 * t + 1] = jnp.where(s0, black, red)[lo:hi]

    loop(l0, 0, l0.block_pairs, last)
    for group in (send_e0, send_f0, send_e1, send_f1):
        sent(group)
    for kind in range(2):
        gather_end(kind)


def per_device(gx, gy, right_side, permittivity):
    bx, by, nz = right_side.shape
    n = gx * gy
    wide = -(-gx * (nz // 4) // 128) * 128
    scratch, names = [], []

    def buffer(owner, name, *shape):
        scratch.append(pltpu.VMEM(shape, F32))
        names.append((owner, name))

    refs = {}
    levels = []
    for index in range(LEVELS):
        level = Level()
        level.index, level.gx = index, gx
        level.zlen = nz >> index
        level.whole = index >= 2
        level.block_x = bx >> index
        if level.whole:
            level.rim_x = level.rim_y = level.rim_pairs = 0
            level.pairs = level.block_pairs = level.block_x // 2
            level.high = level.block_y = (by >> index) * gy
            level.lanes = wide
        else:
            level.rim_x, level.rim_y = 6, 8
            level.block_y = by >> index
            level.rim_pairs, level.block_pairs = level.rim_x // 2, level.block_x // 2
            level.pairs = level.block_pairs + 2 * level.rim_pairs
            level.high = level.block_y + 2 * level.rim_y
            level.lanes = nz
        size = (level.high, level.lanes)
        level.e, level.v = [None, None], [None, None]
        for c in range(2):
            buffer(level.e, c, level.pairs + 2, *size)
            buffer(level.v, c, level.pairs + 2, *size)
        buffer(level, "inv", 2, level.pairs, *size)
        buffer(level, "a", 2, 6, level.pairs, *size)
        if index < 2:
            buffer(None, f"e{index}", 2 * level.pairs, *size)
            buffer(None, f"f{index}", 2 * level.pairs, *size)
            buffer(None, f"vh{index}", 2, level.pairs + 2, *size)
        if index == 2:
            buffer(None, "big", level.pairs, level.lanes // 128, level.high, 128)
            buffer(None, "full", level.block_x, level.high + 16, level.lanes)
        if index > 2:
            buffer(level, "full", level.block_x, *size)
        levels.append(level)
    l0 = levels[0]
    buffer(None, "tmp", l0.pairs, 1, l0.high, l0.lanes)
    groups = levels[2].block_x // (128 // levels[2].zlen)
    buffer(None, "stage", 2, n, groups, 8, 128)
    buffer(None, "packed", 2, groups, 8, 128)
    sems = [
        pltpu.SemaphoreType.DMA((8, 8)),
        pltpu.SemaphoreType.DMA((8, 8)),
        pltpu.SemaphoreType.DMA((2,)),
        pltpu.SemaphoreType.DMA((2,)),
    ]

    def body(right_ref, permit_ref, out_ref, *buffers):
        me_x, me_y = lax.axis_index("gx"), lax.axis_index("gy")
        for (owner, name), ref in zip(names, buffers):
            if owner is None:
                refs[name] = ref
            elif isinstance(owner, list):
                owner[name] = ref
            else:
                setattr(owner, name, ref)
        refs["sems"] = buffers[len(names) :]
        for level in levels:
            if level.whole:
                level.first_x, level.last_x = 0, level.pairs - 1
                level.first_y, level.last_y = 0, level.high - 1
            else:
                level.first_x = level.rim_pairs - me_x * level.block_pairs
                level.last_x = level.first_x + gx * level.block_pairs - 1
                level.first_y = level.rim_y - me_y * level.block_y
                level.last_y = level.first_y + gy * level.block_y - 1
        kernel(gx, gy, right_ref, permit_ref, out_ref, refs, levels)

    return pl.pallas_call(
        body,
        out_shape=jax.ShapeDtypeStruct(right_side.shape, F32),
        in_specs=[pl.BlockSpec(memory_space=pltpu.VMEM)] * 2,
        out_specs=pl.BlockSpec(memory_space=pltpu.VMEM),
        scratch_shapes=scratch + sems,
        compiler_params=pltpu.CompilerParams(
            collective_id=0, has_side_effects=True, vmem_limit_bytes=60 * 2**20
        ),
    )(right_side, permittivity)


def solution(mesh):
    gx, gy = mesh.shape["gx"], mesh.shape["gy"]
    placed = (P("gx", "gy", None), P("gx", "gy", None))
    return jax.shard_map(
        functools.partial(per_device, gx, gy),
        mesh=mesh,
        in_specs=placed,
        out_specs=P("gx", "gy", None),
        check_vma=False,
    )
```

```python
import functools

import jax
import jax.numpy as jnp
from jax import lax
from jax.experimental import pallas as pl
from jax.experimental.pallas import tpu as pltpu
from jax.sharding import PartitionSpec as P

LEVELS = 5
SMOOTH = 2
COARSE_SWEEPS = 12
MESH = pl.DeviceIdType.MESH
F32 = jnp.float32


DIRS = [(dx, dy) for dx in (-1, 0, 1) for dy in (-1, 0, 1) if (dx, dy) != (0, 0)]
DIRS.sort(key=lambda d: (d[0] == 0, d[1] != 0))


class Level:
    pass


def iota(shape, dim):
    return lax.broadcasted_iota(jnp.int32, shape, dim)


def even_mask(rows, lanes):
    return (iota((rows, lanes), 0) + iota((rows, lanes), 1)) % 2 == 0


def roll(x, shift, axis):
    return pltpu.roll(x, shift % x.shape[axis], axis)


def sum_lanes(x, lanes):
    pick = jnp.where(iota((lanes, lanes), 0) // 2 == iota((lanes, lanes), 1), F32(0.125), F32(0.0))
    return jnp.dot(x, pick, precision=lax.Precision.HIGHEST, preferred_element_type=F32)


def spread_lanes(x, lanes):
    pick = jnp.where(iota((lanes, lanes), 0) == iota((lanes, lanes), 1) // 2, F32(1.0), F32(0.0))
    return jnp.dot(x, pick, precision=lax.Precision.HIGHEST, preferred_element_type=F32)


def put_rows(tmp, t, values):
    for h in range(tmp.shape[1]):
        tmp[t, h, 0 : values.shape[-2], :] = values[..., h * 128 : h * 128 + 128]


def get_row(tmp, t, high):
    tiles = [tmp[t, h, 0:high, :] for h in range(tmp.shape[1])]
    return tiles[0] if len(tiles) == 1 else jnp.concatenate(tiles, axis=-1)


def get_strided(tmp, rows, count, first):
    tiles = [tmp[0:rows, h, pl.ds(first, count, 2), :] for h in range(tmp.shape[1])]
    return tiles[0] if len(tiles) == 1 else jnp.concatenate(tiles, axis=-1)


def restrict(tmp, rows, high):
    lanes = tmp.shape[1] * 128
    both = get_strided(tmp, rows, high // 2, 0) + get_strided(tmp, rows, high // 2, 1)
    flat = both.reshape(rows * (high // 2), lanes)
    return sum_lanes(flat, lanes).reshape(rows, high // 2, lanes)


def spread(tmp, coarse):
    rows, high, lanes = coarse.shape
    wide = spread_lanes(coarse.reshape(rows * high, lanes), lanes).reshape(rows, high, lanes)
    for h in range(tmp.shape[1]):
        part = wide[..., h * 128 : h * 128 + 128]
        tmp[0:rows, h, pl.ds(0, high, 2), :] = part
        tmp[0:rows, h, pl.ds(1, high, 2), :] = part


def wrap(level, ref):
    if level.whole:
        ref[0] = roll(ref[level.pairs], level.zlen, 1)
        ref[level.pairs + 1] = roll(ref[1], -level.zlen, 1)


def inverse(x):
    y = pl.reciprocal(x, approx=True)
    y = y * (2.0 - x * y)
    return y * (2.0 - x * y)


def loop(level, lo, hi, body):
    size = min(hi - lo, max(1, 32 * 1024 // (level.high * level.lanes)))
    if size < 1:
        return
    full = (hi - lo) // size

    def step(i, _):
        for k in range(size):
            body(lo + i * size + k)
        return 0

    if full > 1:
        lax.fori_loop(0, full, step, 0)
    else:
        step(0, 0)
    for t in range(lo + full * size, hi):
        body(t)


def reach(level, cells):
    if level.whole:
        return 0, level.pairs
    more = (cells + 1) // 2
    return level.rim_pairs - more, level.rim_pairs + level.block_pairs + more


def pack(level, get, put, lo, hi):
    s = even_mask(level.high, level.lanes)

    def step(t):
        first, second = get(2 * t), get(2 * t + 1)
        put(t, jnp.where(s, first, second), jnp.where(s, second, first))

    loop(level, lo, hi, step)


def put_e(level):
    def put(t, first, second):
        level.e[0][t + 1] = first
        level.e[1][t + 1] = second

    return put


class Ends:
    def __init__(self, level):
        shape = (level.high, level.lanes)
        row, lane = iota(shape, 0), iota(shape, 1)
        self.level = level
        self.s = even_mask(*shape)
        self.low_y, self.top_y = row == level.first_y, row == level.last_y
        self.low_z = lane % level.zlen == 0
        self.top_z = lane % level.zlen == level.zlen - 1
        if level.whole:
            self.low_x = lane < level.zlen
            self.top_x = (lane >= (level.gx - 1) * level.zlen) & (lane < level.gx * level.zlen)

    def beyond(self, c, t):
        level = self.level
        even = self.s if c == 0 else ~self.s
        at_low = jnp.asarray(t == level.first_x).astype(jnp.int32)
        at_top = jnp.asarray(t == level.last_x).astype(jnp.int32)
        out = jnp.where(even, at_low, at_top) > 0
        if level.whole:
            out = out & ((even & self.low_x) | (~even & self.top_x))
        return out


def finish(level, ends, c, t, w, beyond):
    total = ((w[0] + w[1]) + (w[2] + w[3])) + (w[4] + w[5])
    inv = inverse(total)
    level.inv[c, t] = inv
    w = list(w)
    w[1] = jnp.where(beyond, 0.0, w[1])
    w[2] = jnp.where(ends.top_y, 0.0, w[2])
    w[3] = jnp.where(ends.low_y, 0.0, w[3])
    for k in range(6):
        level.a[c, k, t] = w[k] * inv


def red_weights(level, ends, lo, hi):
    scale = F32(2.0 * 0.25**level.index)
    end_scale = F32(0.25**level.index)
    s = ends.s

    def step(t):
        own, other = level.e[0][t + 1], level.e[1][t + 1]
        outer = jnp.where(s, level.e[1][t], level.e[1][t + 2])
        scaled, end = scale * own, end_scale * own
        beyond = ends.beyond(0, t)

        def weight(n):
            return scaled * n * inverse(own + n)

        w = [
            weight(other),
            weight(outer),
            weight(roll(other, -1, 0)),
            weight(roll(other, 1, 0)),
            jnp.where(ends.top_z, 0.0, weight(roll(other, -1, 1))),
            jnp.where(ends.low_z, 0.0, weight(roll(other, 1, 1))),
        ]
        level.v[0][t + 1] = w[1]
        level.a[1, 0, t] = w[0]
        level.a[1, 2, t] = roll(w[3], -1, 0)
        level.a[1, 3, t] = roll(w[2], 1, 0)
        level.a[1, 4, t] = roll(w[5], -1, 1)
        level.a[1, 5, t] = roll(w[4], 1, 1)
        w[1] = jnp.where(beyond, end, w[1])
        w[2] = jnp.where(ends.top_y, end, w[2])
        w[3] = jnp.where(ends.low_y, end, w[3])
        finish(level, ends, 0, t, w, beyond)

    lax.fori_loop(lo, hi, lambda t, c: (step(t), c)[1], 0)


def black_weights(level, ends, lo, hi):
    end_scale = F32(0.25**level.index)

    def step(t):
        end = end_scale * level.e[1][t + 1]
        beyond = ends.beyond(1, t)
        w = [level.a[1, k, t] for k in (0, 0, 2, 3, 4, 5)]
        w[1] = jnp.where(ends.s, level.v[0][t + 2], level.v[0][t])
        w[1] = jnp.where(beyond, end, w[1])
        w[2] = jnp.where(ends.top_y, end, w[2])
        w[3] = jnp.where(ends.low_y, end, w[3])
        finish(level, ends, 1, t, w, beyond)

    lax.fori_loop(lo, hi, lambda t, c: (step(t), c)[1], 0)


def coefficients(level, cells):
    ends = Ends(level)
    lo, hi = reach(level, cells)
    more = 0 if level.whole else 1
    red_weights(level, ends, lo - more, hi + more)
    wrap(level, level.v[0])
    black_weights(level, ends, lo, hi)


def updated(level, c, t, s):
    v, a = level.v[1 - c], level.a
    other = v[t + 1]
    even = s if c == 0 else ~s
    outer = jnp.where(even, v[t], v[t + 2])
    x = level.e[c][t + 1] + a[c, 0, t] * other + a[c, 1, t] * outer
    y = a[c, 2, t] * roll(other, -1, 0) + a[c, 3, t] * roll(other, 1, 0)
    z = a[c, 4, t] * roll(other, -1, 1) + a[c, 5, t] * roll(other, 1, 1)
    return x + (y + z)


def half_sweep(level, c, cells):
    s = even_mask(level.high, level.lanes)

    def step(t):
        level.v[c][t + 1] = updated(level, c, t, s)

    loop(level, *reach(level, cells), step)
    wrap(level, level.v[c])


def sweeps(level, count, cells):
    for k in range(2 * count):
        half_sweep(level, k % 2, cells + 2 * count - 1 - k)


def start(level, get, cells, keep):
    def put(t, first, second):
        red = first * level.inv[0, t]
        level.e[0][t + 1] = red
        level.v[0][t + 1] = red
        level.e[1][t + 1] = second * level.inv[1, t]

    pack(level, get, put, *reach(level, keep))
    wrap(level, level.v[0])
    if cells is not None:
        half_sweep(level, 1, cells)


def solve_small(level, count):
    s = even_mask(level.high, level.lanes)
    a = [[level.a[c, k, 0] for k in range(6)] for c in range(2)]
    f = [level.e[c][1] for c in range(2)]

    def half(c, other):
        even = s if c == 0 else ~s
        outer = jnp.where(even, roll(other, level.zlen, 1), roll(other, -level.zlen, 1))
        x = f[c] + a[c][0] * other + a[c][1] * outer
        y = a[c][2] * roll(other, -1, 0) + a[c][3] * roll(other, 1, 0)
        z = a[c][4] * roll(other, -1, 1) + a[c][5] * roll(other, 1, 1)
        return x + (y + z)

    def step(_, v):
        red = half(0, v[1])
        return red, half(1, red)

    first = f[0]
    v = lax.fori_loop(0, count - 1, step, (first, half(1, first)))
    for c in range(2):
        level.v[c][1] = v[c]


def residual_sums(level, tmp):
    s = even_mask(level.high, level.lanes)
    lo, hi = reach(level, 0)
    ylo, high = level.rim_y, level.block_y

    def step(t):
        r = (updated(level, 0, t, s) - level.v[0][t + 1]) * inverse(level.inv[0, t])
        put_rows(tmp, t - lo, r[ylo : ylo + high])

    loop(level, lo, hi, step)


def coarse_row(level, s, x):
    red, black = level.v[0][x // 2 + 1], level.v[1][x // 2 + 1]
    return jnp.where(s, red, black) if x % 2 == 0 else jnp.where(s, black, red)


def kernel(gx, gy, right_ref, permit_ref, out_ref, refs, lv):
    me_x, me_y = lax.axis_index("gx"), lax.axis_index("gy")
    l0, l1, l2, l3, l4 = lv
    send_sem, recv_sem, all_send, all_recv, local = refs["sems"]

    def inside(dx, dy):
        x, y = me_x + dx, me_y + dy
        return (x >= 0) & (x < gx) & (y >= 0) & (y < gy)

    def cut(d, size, rim, block):
        if d == 0:
            return pl.ds(rim, block), pl.ds(rim, block)
        if d == 1:
            return pl.ds(rim + block - size, size), pl.ds(rim - size, size)
        return pl.ds(rim, size), pl.ds(rim + block, size)

    def copies(kind, src, dst, width, geometry):
        rim_x, block_x, rim_y, block_y = geometry
        out = []
        for k, (dx, dy) in enumerate(DIRS):
            sx, tx = cut(dx, width, rim_x, block_x)
            sy, ty = cut(dy, 8, rim_y, block_y)
            copy = pltpu.make_async_remote_copy(
                src_ref=src.at[sx, sy],
                dst_ref=dst.at[tx, ty],
                send_sem=send_sem.at[kind, k],
                recv_sem=recv_sem.at[kind, k],
                device_id=(me_x + dx, me_y + dy),
                device_id_type=MESH,
            )
            out.append((dx, dy, copy))
        return out

    def go(group):
        for dx, dy, copy in group:
            pl.when(inside(dx, dy))(copy.start)

    def arrive(group):
        for dx, dy, copy in group:
            pl.when(inside(-dx, -dy))(copy.wait_recv)

    def sent(group):
        for dx, dy, copy in group:
            pl.when(inside(dx, dy))(copy.wait_send)

    e0, f0, e1, f1 = refs["e0"], refs["f0"], refs["e1"], refs["f1"]
    vh0, vh1 = refs["vh0"], refs["vh1"]
    g0, g1 = (l0.rim_x, l0.block_x, l0.rim_y, l0.block_y), (l1.rim_x, l1.block_x, l1.rim_y, l1.block_y)
    p0, p1 = (l0.rim_pairs + 1, l0.block_pairs) + g0[2:], (l1.rim_pairs + 1, l1.block_pairs) + g1[2:]
    deep = 2 * SMOOTH
    send_e0 = copies(0, e0, e0, deep + 1, g0)
    send_f0 = copies(1, f0, f0, deep, g0)
    send_e1 = copies(2, e1, e1, deep + 2, g1)
    send_f1 = copies(3, f1, f1, deep + 1, g1)
    send_v0, send_v1 = [], []
    for c in range(2):
        send_v0 += copies(4 + c, l0.v[c], vh0.at[c], deep // 2, p0)
        send_v1 += copies(6 + c, l1.v[c], vh1.at[c], deep // 2 + 1, p1)

    x0, y0 = pl.ds(l0.rim_x, l0.block_x), pl.ds(l0.rim_y, l0.block_y)
    load_e = pltpu.make_async_copy(permit_ref, e0.at[x0, y0, :], local.at[0])
    load_f = pltpu.make_async_copy(right_ref, f0.at[x0, y0, :], local.at[1])
    load_e.start()
    load_f.start()

    def fill(ref, lead, value, geometry):
        rim_x, block_x, rim_y, block_y = geometry
        rows, high, width = ref.shape[-3:]
        top_x, top_y = rim_x + block_x, rim_y + block_y
        for xs, ys in (
            ((0, rim_x), (0, high)),
            ((top_x, rows), (0, high)),
            ((rim_x, top_x), (0, rim_y)),
            ((rim_x, top_x), (top_y, high)),
        ):
            part = jnp.full((xs[1] - xs[0], ys[1] - ys[0], width), value, F32)
            ref[lead + (slice(*xs), slice(*ys))] = part

    fill(e0, (), 1.0, g0)
    fill(f0, (), 0.0, g0)
    fill(e1, (), 1.0, g1)
    fill(f1, (), 0.0, g1)
    for c in range(2):
        fill(vh0, (c,), 0.0, p0)
        fill(vh1, (c,), 0.0, p1)
    barrier = pltpu.get_barrier_semaphore()

    def in_x(d):
        return (lax.rem(me_x + d, gx), me_y)

    def in_y(d):
        return (me_x, lax.rem(me_y + d, gy))

    def greet(to, count):
        def step(d, carry):
            pl.semaphore_signal(barrier, inc=1, device_id=to(d), device_id_type=MESH)
            return carry

        lax.fori_loop(1, count, step, 0)

    greet(in_x, gx)
    greet(in_y, gy)
    guests = jnp.int32(gx - 1 + gy - 1)
    for dx, dy in DIRS:
        if dx != 0 and dy != 0:

            @pl.when(inside(dx, dy))
            def _():
                pl.semaphore_signal(
                    barrier, inc=1, device_id=(me_x + dx, me_y + dy), device_id_type=MESH
                )

            guests = guests + inside(dx, dy).astype(jnp.int32)
    for level in (l0, l1):
        for c in range(2):
            for t in list(range(3)) + list(range(level.pairs - 1, level.pairs + 2)):
                level.v[c][t] = jnp.zeros((level.high, level.lanes), F32)
            for t in (0, level.pairs + 1):
                level.e[c][t] = jnp.ones((level.high, level.lanes), F32)
    pl.semaphore_wait(barrier, guests)

    load_e.wait()
    go(send_e0)
    load_f.wait()
    go(send_f0)

    tmp = refs["tmp"]
    lanes = l0.lanes

    def narrow(values, used, other):
        lane = iota(values.shape, len(values.shape) - 1)
        return jnp.where(lane < used, values, F32(other))

    put_rows(
        tmp,
        pl.ds(0, l1.block_x),
        e0[x0, y0, :].reshape(l1.block_x, 2, l0.block_y, lanes).sum(axis=1),
    )
    own_e1 = narrow(restrict(tmp, l1.block_x, l0.block_y), l1.zlen, 1.0)
    e1[pl.ds(l1.rim_x, l1.block_x), pl.ds(l1.rim_y, l1.block_y), :] = own_e1

    block2, z2 = l2.block_x, l2.zlen
    per = 128 // z2
    groups = block2 // per

    def gather_start(kind, rows):
        stage, packed = refs["stage"].at[kind], refs["packed"].at[kind]
        group = iota((8, 128), 1) // z2
        for g in range(groups):
            value = rows[g * per]
            for k in range(1, per):
                value = jnp.where(group == k, roll(rows[g * per + k], k * z2, 1), value)
            packed[g] = value
            stage[me_y, me_x, g] = value

        gather_line(kind, 0, in_x, gx, packed, stage.at[me_y, me_x])

    def gather_line(kind, stop, to, count, src, dst):
        def step(d, carry):
            pltpu.make_async_remote_copy(
                src_ref=src,
                dst_ref=dst,
                send_sem=all_send.at[kind, stop],
                recv_sem=all_recv.at[kind, stop],
                device_id=to(d),
                device_id_type=MESH,
            ).start()
            return carry

        lax.fori_loop(1, count, step, 0)

    def gather_next(kind):
        stage = refs["stage"].at[kind]
        others = stage.at[me_y, pl.ds(0, gx - 1)]
        pltpu.make_async_copy(others, others, all_recv.at[kind, 0]).wait()
        gather_line(kind, 1, in_y, gy, stage.at[me_y], stage.at[me_y])

    def gather_wait(kind, full):
        stage = refs["stage"].at[kind]
        others = stage.at[pl.ds(0, gy - 1)]
        pltpu.make_async_copy(others, others, all_recv.at[kind, 1]).wait()
        group = iota((8, 128), 1) // z2

        def step(q, _):
            for x in range(block2):
                tiles = []
                for h in range(full.shape[-1] // 128):
                    value = None
                    for k in range(per):
                        p = h * per + k
                        if p >= gx:
                            break
                        part = roll(stage[q, p, x // per], (k - x % per) * z2, 1)
                        value = part if k == 0 else jnp.where(group == k, part, value)
                    tiles.append(value)
                row = tiles[0] if len(tiles) == 1 else jnp.concatenate(tiles, axis=1)
                full[x, pl.ds(pl.multiple_of(q * 8 + 8, 8), 8), :] = row
            return 0

        lax.fori_loop(0, gy, step, 0)

    def gather_end(kind):
        others = refs["stage"].at[kind, 0, pl.ds(0, gx - 1)]
        pltpu.make_async_copy(others, others, all_send.at[kind, 0]).wait()
        others = refs["stage"].at[kind, pl.ds(0, gy - 1)]
        pltpu.make_async_copy(others, others, all_send.at[kind, 1]).wait()

    put_rows(tmp, pl.ds(0, block2), own_e1.reshape(block2, 2, l1.block_y, lanes).sum(axis=1))
    own_e2 = restrict(tmp, block2, l1.block_y)

    arrive([item for item in send_e0 if item[0] == 0])
    lo, hi = reach(l0, 0)
    ends = Ends(l0)
    pack(l0, lambda x: e0[x], put_e(l0), lo, hi)
    red_weights(l0, ends, lo + 1, hi - 1)
    black_weights(l0, ends, lo + 2, hi - 2)
    arrive([item for item in send_e0 if item[0] != 0])
    gather_start(0, own_e2)
    go(send_e1)
    far_lo, far_hi = reach(l0, deep)
    pack(l0, lambda x: e0[x], put_e(l0), 0, lo)
    pack(l0, lambda x: e0[x], put_e(l0), hi, l0.pairs)
    red_weights(l0, ends, far_lo - 1, lo + 1)
    red_weights(l0, ends, hi - 1, far_hi + 1)
    black_weights(l0, ends, far_lo, lo + 2)
    black_weights(l0, ends, hi - 2, far_hi)
    arrive(send_f0)
    start(l0, lambda x: f0[x], deep - 1, deep)
    sweeps(l0, SMOOTH - 1, 1)
    residual_sums(l0, tmp)
    f1[pl.ds(l1.rim_x, l1.block_x), pl.ds(l1.rim_y, l1.block_y), :] = restrict(
        tmp, l1.block_x, l0.block_y
    )
    go(send_f1)
    gather_next(0)

    arrive(send_e1)
    pack(l1, lambda x: e1[x], put_e(l1), 0, l1.pairs)
    coefficients(l1, deep)
    arrive(send_f1)
    start(l1, lambda x: f1[x], deep - 1, deep + 1)
    sweeps(l1, SMOOTH - 1, 1)
    residual_sums(l1, tmp)
    gather_start(1, restrict(tmp, block2, l1.block_y))

    full, big = refs["full"], refs["big"]
    full[...] = jnp.zeros(full.shape, F32)
    gather_wait(0, full)
    gather_next(1)
    pack(l2, lambda x: full[x, 8 : 8 + l2.high], put_e(l2), 0, l2.pairs)
    for fine, coarse in ((l2, l3), (l3, l4)):
        for c in range(2):
            wrap(fine, fine.e[c])
        coefficients(fine, 0)
        for t in range(fine.pairs):
            put_rows(big, t, fine.e[0][t + 1] + fine.e[1][t + 1])
        rows = narrow(restrict(big, fine.pairs, fine.high), gx * coarse.zlen, 1.0)
        coarse.full[...] = rows
        pack(coarse, lambda x: coarse.full[x], put_e(coarse), 0, coarse.pairs)
    for c in range(2):
        wrap(l4, l4.e[c])
    coefficients(l4, 0)

    gather_wait(1, full)
    go(send_v1)
    go(send_v0)
    start(l2, lambda x: full[x, 8 : 8 + l2.high], 0, 0)
    sweeps(l2, SMOOTH - 1, 0)
    for fine, coarse in ((l2, l3), (l3, l4)):
        residual_sums(fine, big)
        coarse.full[...] = restrict(big, fine.pairs, fine.high)
        small = coarse is l4 and coarse.pairs == 1
        start(coarse, lambda x: coarse.full[x], None if small else 0, 0)
        if small:
            solve_small(coarse, COARSE_SWEEPS)
        else:
            sweeps(coarse, SMOOTH - 1 if coarse is l3 else COARSE_SWEEPS - 1, 0)

    def correct(fine, coarse):
        s = even_mask(coarse.high, coarse.lanes)
        spread(big, jnp.stack([coarse_row(coarse, s, t) for t in range(fine.pairs)]))
        for c in range(2):
            for t in range(fine.pairs):
                fine.v[c][t + 1] = fine.v[c][t + 1] + get_row(big, t, fine.high)
            wrap(fine, fine.v[c])
        sweeps(fine, SMOOTH, 0)

    correct(l3, l4)
    correct(l2, l3)

    def add(level, halo, far_lo, far_hi):
        lo, hi = reach(level, 0)
        ylo, yhi = level.rim_y, level.rim_y + level.block_y
        for c in range(2):
            for t in list(range(far_lo, lo)) + list(range(hi, far_hi)):
                level.v[c][t + 1] = halo[c, t + 1] + get_row(tmp, t - far_lo, level.high)

            def step(t):
                row = jnp.concatenate(
                    [
                        halo[c, t + 1, 0:ylo],
                        level.v[c][t + 1, ylo:yhi],
                        halo[c, t + 1, yhi : level.high],
                    ],
                    axis=0,
                )
                level.v[c][t + 1] = row + get_row(tmp, t - far_lo, level.high)

            loop(level, lo, hi, step)

    s2 = even_mask(l2.high, l2.lanes)
    for x in range(block2):
        full[x, 8 : 8 + l2.high, :] = coarse_row(l2, s2, x)
    rows = []
    high = l1.high // 2
    skip = 8 - l1.rim_y // 2
    for t in range(l1.pairs):
        x = t - l1.rim_pairs
        p = lax.rem(me_x + x // block2 + gx, gx)
        value = full[x % block2, pl.ds(pl.multiple_of(me_y * 8, 8), 24), :]
        value = pltpu.roll(value, lax.rem(l2.lanes - p * z2, l2.lanes), 1)
        rows.append(value[skip : skip + high, 0:128])
    arrive(send_v1)
    sent(send_v1)
    spread(tmp, jnp.stack(rows))
    add(l1, vh1, 0, l1.pairs)
    sweeps(l1, SMOOTH, 2)

    s1 = even_mask(l1.high, l1.lanes)
    first = l1.rim_x - l0.rim_pairs
    low = l1.rim_y - l0.rim_y // 2
    far_lo, far_hi = reach(l0, deep)
    rows = [coarse_row(l1, s1, first + t)[low : low + l0.high // 2] for t in range(far_lo, far_hi)]
    arrive(send_v0)
    sent(send_v0)
    spread(tmp, jnp.stack(rows))
    add(l0, vh0, far_lo, far_hi)
    sweeps(l0, SMOOTH, 0)

    s0 = even_mask(l0.high, l0.lanes)

    def last(t):
        red, black = l0.v[0][t + l0.rim_pairs + 1], l0.v[1][t + l0.rim_pairs + 1]
        lo, hi = l0.rim_y, l0.rim_y + l0.block_y
        out_ref[2 * t] = jnp.where(s0, red, black)[lo:hi]
        out_ref[2 * t + 1] = jnp.where(s0, black, red)[lo:hi]

    loop(l0, 0, l0.block_pairs, last)
    for group in (send_e0, send_f0, send_e1, send_f1):
        sent(group)
    for kind in range(2):
        gather_end(kind)


def per_device(gx, gy, right_side, permittivity):
    bx, by, nz = right_side.shape
    wide = -(-gx * (nz // 4) // 128) * 128
    scratch, names = [], []

    def buffer(owner, name, *shape):
        scratch.append(pltpu.VMEM(shape, F32))
        names.append((owner, name))

    refs = {}
    levels = []
    for index in range(LEVELS):
        level = Level()
        level.index, level.gx = index, gx
        level.zlen = nz >> index
        level.whole = index >= 2
        level.block_x = bx >> index
        if level.whole:
            level.rim_x = level.rim_y = level.rim_pairs = 0
            level.pairs = level.block_pairs = level.block_x // 2
            level.high = level.block_y = (by >> index) * gy
            level.lanes = wide
        else:
            level.rim_x, level.rim_y = 6, 8
            level.block_y = by >> index
            level.rim_pairs, level.block_pairs = level.rim_x // 2, level.block_x // 2
            level.pairs = level.block_pairs + 2 * level.rim_pairs
            level.high = level.block_y + 2 * level.rim_y
            level.lanes = nz
        size = (level.high, level.lanes)
        level.e, level.v = [None, None], [None, None]
        for c in range(2):
            buffer(level.e, c, level.pairs + 2, *size)
            buffer(level.v, c, level.pairs + 2, *size)
        buffer(level, "inv", 2, level.pairs, *size)
        buffer(level, "a", 2, 6, level.pairs, *size)
        if index < 2:
            buffer(None, f"e{index}", 2 * level.pairs, *size)
            buffer(None, f"f{index}", 2 * level.pairs, *size)
            buffer(None, f"vh{index}", 2, level.pairs + 2, *size)
        if index == 2:
            buffer(None, "big", level.pairs, level.lanes // 128, level.high, 128)
            buffer(None, "full", level.block_x, level.high + 16, level.lanes)
        if index > 2:
            buffer(level, "full", level.block_x, *size)
        levels.append(level)
    l0 = levels[0]
    buffer(None, "tmp", l0.pairs, 1, l0.high, l0.lanes)
    groups = levels[2].block_x // (128 // levels[2].zlen)
    buffer(None, "stage", 2, gy, gx, groups, 8, 128)
    buffer(None, "packed", 2, groups, 8, 128)
    sems = [
        pltpu.SemaphoreType.DMA((8, 8)),
        pltpu.SemaphoreType.DMA((8, 8)),
        pltpu.SemaphoreType.DMA((2, 2)),
        pltpu.SemaphoreType.DMA((2, 2)),
        pltpu.SemaphoreType.DMA((2,)),
    ]

    def body(right_ref, permit_ref, out_ref, *buffers):
        me_x, me_y = lax.axis_index("gx"), lax.axis_index("gy")
        for (owner, name), ref in zip(names, buffers):
            if owner is None:
                refs[name] = ref
            elif isinstance(owner, list):
                owner[name] = ref
            else:
                setattr(owner, name, ref)
        refs["sems"] = buffers[len(names) :]
        for level in levels:
            if level.whole:
                level.first_x, level.last_x = 0, level.pairs - 1
                level.first_y, level.last_y = 0, level.high - 1
            else:
                level.first_x = level.rim_pairs - me_x * level.block_pairs
                level.last_x = level.first_x + gx * level.block_pairs - 1
                level.first_y = level.rim_y - me_y * level.block_y
                level.last_y = level.first_y + gy * level.block_y - 1
        kernel(gx, gy, right_ref, permit_ref, out_ref, refs, levels)

    return pl.pallas_call(
        body,
        out_shape=jax.ShapeDtypeStruct(right_side.shape, F32),
        in_specs=[pl.BlockSpec(memory_space=pl.ANY)] * 2,
        out_specs=pl.BlockSpec(memory_space=pltpu.VMEM),
        scratch_shapes=scratch + sems,
        compiler_params=pltpu.CompilerParams(
            collective_id=0, has_side_effects=True, vmem_limit_bytes=60 * 2**20
        ),
    )(right_side, permittivity)


def solution(mesh):
    gx, gy = mesh.shape["gx"], mesh.shape["gy"]
    placed = (P("gx", "gy", None), P("gx", "gy", None))
    return jax.shard_map(
        functools.partial(per_device, gx, gy),
        mesh=mesh,
        in_specs=placed,
        out_specs=P("gx", "gy", None),
        check_vma=False,
    )
```

```python
import functools

import jax
import jax.numpy as jnp
from jax import lax
from jax.experimental import pallas as pl
from jax.experimental.pallas import tpu as pltpu
from jax.sharding import PartitionSpec as P

LEVELS = 5
SMOOTH = 2
COARSE_SWEEPS = 12
MESH = pl.DeviceIdType.MESH
F32 = jnp.float32


DIRS = [(dx, dy) for dx in (-1, 0, 1) for dy in (-1, 0, 1) if (dx, dy) != (0, 0)]
DIRS.sort(key=lambda d: (d[0] == 0, d[1] != 0))


class Level:
    pass


def iota(shape, dim):
    return lax.broadcasted_iota(jnp.int32, shape, dim)


def even_mask(rows, lanes):
    return (iota((rows, lanes), 0) + iota((rows, lanes), 1)) % 2 == 0


def roll(x, shift, axis):
    return pltpu.roll(x, shift % x.shape[axis], axis)


def sum_lanes(x, lanes):
    pick = jnp.where(iota((lanes, lanes), 0) // 2 == iota((lanes, lanes), 1), F32(0.125), F32(0.0))
    return jnp.dot(x, pick, precision=lax.Precision.HIGHEST, preferred_element_type=F32)


def spread_lanes(x, lanes):
    pick = jnp.where(iota((lanes, lanes), 0) == iota((lanes, lanes), 1) // 2, F32(1.0), F32(0.0))
    return jnp.dot(x, pick, precision=lax.Precision.HIGHEST, preferred_element_type=F32)


def put_rows(tmp, t, values):
    for h in range(tmp.shape[1]):
        tmp[t, h, 0 : values.shape[-2], :] = values[..., h * 128 : h * 128 + 128]


def get_row(tmp, t, high):
    tiles = [tmp[t, h, 0:high, :] for h in range(tmp.shape[1])]
    return tiles[0] if len(tiles) == 1 else jnp.concatenate(tiles, axis=-1)


def get_strided(tmp, rows, count, first):
    tiles = [tmp[0:rows, h, pl.ds(first, count, 2), :] for h in range(tmp.shape[1])]
    return tiles[0] if len(tiles) == 1 else jnp.concatenate(tiles, axis=-1)


def restrict(tmp, rows, high):
    lanes = tmp.shape[1] * 128
    both = get_strided(tmp, rows, high // 2, 0) + get_strided(tmp, rows, high // 2, 1)
    flat = both.reshape(rows * (high // 2), lanes)
    return sum_lanes(flat, lanes).reshape(rows, high // 2, lanes)


def spread(tmp, coarse):
    rows, high, lanes = coarse.shape
    wide = spread_lanes(coarse.reshape(rows * high, lanes), lanes).reshape(rows, high, lanes)
    for h in range(tmp.shape[1]):
        part = wide[..., h * 128 : h * 128 + 128]
        tmp[0:rows, h, pl.ds(0, high, 2), :] = part
        tmp[0:rows, h, pl.ds(1, high, 2), :] = part


def wrap(level, ref):
    if level.whole:
        ref[0] = roll(ref[level.pairs], level.zlen, 1)
        ref[level.pairs + 1] = roll(ref[1], -level.zlen, 1)


def inverse(x):
    y = pl.reciprocal(x, approx=True)
    y = y * (2.0 - x * y)
    return y * (2.0 - x * y)


def loop(level, lo, hi, body):
    size = min(hi - lo, max(1, 32 * 1024 // (level.high * level.lanes)))
    if size < 1:
        return
    full = (hi - lo) // size

    def step(i, _):
        for k in range(size):
            body(lo + i * size + k)
        return 0

    if full > 1:
        lax.fori_loop(0, full, step, 0)
    else:
        step(0, 0)
    for t in range(lo + full * size, hi):
        body(t)


def reach(level, cells):
    if level.whole:
        return 0, level.pairs
    more = (cells + 1) // 2
    return level.rim_pairs - more, level.rim_pairs + level.block_pairs + more


def pack(level, get, put, lo, hi):
    s = even_mask(level.high, level.lanes)

    def step(t):
        first, second = get(2 * t), get(2 * t + 1)
        put(t, jnp.where(s, first, second), jnp.where(s, second, first))

    loop(level, lo, hi, step)


def put_e(level):
    def put(t, first, second):
        level.e[0][t + 1] = first
        level.e[1][t + 1] = second

    return put


class Ends:
    def __init__(self, level):
        shape = (level.high, level.lanes)
        row, lane = iota(shape, 0), iota(shape, 1)
        self.level = level
        self.s = even_mask(*shape)
        self.low_y, self.top_y = row == level.first_y, row == level.last_y
        self.low_z = lane % level.zlen == 0
        self.top_z = lane % level.zlen == level.zlen - 1
        if level.whole:
            self.low_x = lane < level.zlen
            self.top_x = (lane >= (level.gx - 1) * level.zlen) & (lane < level.gx * level.zlen)

    def beyond(self, c, t):
        level = self.level
        even = self.s if c == 0 else ~self.s
        at_low = jnp.asarray(t == level.first_x).astype(jnp.int32)
        at_top = jnp.asarray(t == level.last_x).astype(jnp.int32)
        out = jnp.where(even, at_low, at_top) > 0
        if level.whole:
            out = out & ((even & self.low_x) | (~even & self.top_x))
        return out


def finish(level, ends, c, t, w, beyond):
    total = ((w[0] + w[1]) + (w[2] + w[3])) + (w[4] + w[5])
    inv = inverse(total)
    level.inv[c, t] = inv
    w = list(w)
    w[1] = jnp.where(beyond, 0.0, w[1])
    w[2] = jnp.where(ends.top_y, 0.0, w[2])
    w[3] = jnp.where(ends.low_y, 0.0, w[3])
    for k in range(6):
        level.a[c, k, t] = w[k] * inv


def red_weights(level, ends, lo, hi):
    scale = F32(2.0 * 0.25**level.index)
    end_scale = F32(0.25**level.index)
    s = ends.s

    def step(t):
        own, other = level.e[0][t + 1], level.e[1][t + 1]
        outer = jnp.where(s, level.e[1][t], level.e[1][t + 2])
        scaled, end = scale * own, end_scale * own
        beyond = ends.beyond(0, t)

        def weight(n):
            return scaled * n * inverse(own + n)

        w = [
            weight(other),
            weight(outer),
            weight(roll(other, -1, 0)),
            weight(roll(other, 1, 0)),
            jnp.where(ends.top_z, 0.0, weight(roll(other, -1, 1))),
            jnp.where(ends.low_z, 0.0, weight(roll(other, 1, 1))),
        ]
        level.v[0][t + 1] = w[1]
        level.a[1, 0, t] = w[0]
        level.a[1, 2, t] = roll(w[3], -1, 0)
        level.a[1, 3, t] = roll(w[2], 1, 0)
        level.a[1, 4, t] = roll(w[5], -1, 1)
        level.a[1, 5, t] = roll(w[4], 1, 1)
        w[1] = jnp.where(beyond, end, w[1])
        w[2] = jnp.where(ends.top_y, end, w[2])
        w[3] = jnp.where(ends.low_y, end, w[3])
        finish(level, ends, 0, t, w, beyond)

    lax.fori_loop(lo, hi, lambda t, c: (step(t), c)[1], 0)


def black_weights(level, ends, lo, hi):
    end_scale = F32(0.25**level.index)

    def step(t):
        end = end_scale * level.e[1][t + 1]
        beyond = ends.beyond(1, t)
        w = [level.a[1, k, t] for k in (0, 0, 2, 3, 4, 5)]
        w[1] = jnp.where(ends.s, level.v[0][t + 2], level.v[0][t])
        w[1] = jnp.where(beyond, end, w[1])
        w[2] = jnp.where(ends.top_y, end, w[2])
        w[3] = jnp.where(ends.low_y, end, w[3])
        finish(level, ends, 1, t, w, beyond)

    lax.fori_loop(lo, hi, lambda t, c: (step(t), c)[1], 0)


def coefficients(level, cells):
    ends = Ends(level)
    lo, hi = reach(level, cells)
    more = 0 if level.whole else 1
    red_weights(level, ends, lo - more, hi + more)
    wrap(level, level.v[0])
    black_weights(level, ends, lo, hi)


def updated(level, c, t, s, cut):
    v, a, rows = level.v[1 - c], level.a, slice(*cut)
    other = v[t + 1]
    even = s if c == 0 else ~s
    if level.straight:
        lower = v[t] if t > 0 else roll(v[level.pairs], level.zlen, 1)
        upper = v[t + 2] if t + 1 < level.pairs else roll(v[1], -level.zlen, 1)
    else:
        lower, upper = v[t], v[t + 2]
    outer = jnp.where(even, lower, upper)
    x = level.e[c][t + 1, rows] + a[c, 0, t, rows] * other[rows] + a[c, 1, t, rows] * outer[rows]
    y = a[c, 2, t, rows] * roll(other, -1, 0)[rows] + a[c, 3, t, rows] * roll(other, 1, 0)[rows]
    inner = other[rows]
    z = a[c, 4, t, rows] * roll(inner, -1, 1) + a[c, 5, t, rows] * roll(inner, 1, 1)
    return x + (y + z)


def wrap_values(level, c):
    if not level.straight:
        wrap(level, level.v[c])


def half_sweep(level, c, cells):
    s = even_mask(level.high, level.lanes)
    cut = (0, level.high)
    if cells == 0:
        cut = (level.rim_y, level.rim_y + level.block_y)

    def step(t):
        level.v[c][t + 1, cut[0] : cut[1]] = updated(level, c, t, s, cut)

    loop(level, *reach(level, cells), step)
    wrap_values(level, c)


def sweeps(level, count, cells):
    for k in range(2 * count):
        half_sweep(level, k % 2, cells + 2 * count - 1 - k)


def start(level, get, cells, keep):
    def put(t, first, second):
        red = first * level.inv[0, t]
        level.e[0][t + 1] = red
        level.v[0][t + 1] = red
        level.e[1][t + 1] = second * level.inv[1, t]

    pack(level, get, put, *reach(level, keep))
    wrap_values(level, 0)
    if cells is not None:
        half_sweep(level, 1, cells)


def solve_small(level, count):
    s = even_mask(level.high, level.lanes)
    a = [[level.a[c, k, 0] for k in range(6)] for c in range(2)]
    f = [level.e[c][1] for c in range(2)]

    def half(c, other):
        even = s if c == 0 else ~s
        outer = jnp.where(even, roll(other, level.zlen, 1), roll(other, -level.zlen, 1))
        x = f[c] + a[c][0] * other + a[c][1] * outer
        y = a[c][2] * roll(other, -1, 0) + a[c][3] * roll(other, 1, 0)
        z = a[c][4] * roll(other, -1, 1) + a[c][5] * roll(other, 1, 1)
        return x + (y + z)

    def step(_, v):
        red = half(0, v[1])
        return red, half(1, red)

    first = f[0]
    v = lax.fori_loop(0, count - 1, step, (first, half(1, first)))
    for c in range(2):
        level.v[c][1] = v[c]


def residual_sums(level, tmp):
    s = even_mask(level.high, level.lanes)
    lo, hi = reach(level, 0)
    cut = (level.rim_y, level.rim_y + level.block_y)
    rows = slice(*cut)

    def step(t):
        change = updated(level, 0, t, s, cut) - level.v[0][t + 1, rows]
        put_rows(tmp, t - lo, change * inverse(level.inv[0, t, rows]))

    loop(level, lo, hi, step)


def coarse_row(level, s, x):
    red, black = level.v[0][x // 2 + 1], level.v[1][x // 2 + 1]
    return jnp.where(s, red, black) if x % 2 == 0 else jnp.where(s, black, red)


def kernel(gx, gy, right_ref, permit_ref, out_ref, refs, lv):
    me_x, me_y = lax.axis_index("gx"), lax.axis_index("gy")
    l0, l1, l2, l3, l4 = lv
    send_sem, recv_sem, all_send, all_recv, local = refs["sems"]

    def inside(dx, dy):
        x, y = me_x + dx, me_y + dy
        return (x >= 0) & (x < gx) & (y >= 0) & (y < gy)

    def cut(d, size, rim, block):
        if d == 0:
            return pl.ds(rim, block), pl.ds(rim, block)
        if d == 1:
            return pl.ds(rim + block - size, size), pl.ds(rim - size, size)
        return pl.ds(rim, size), pl.ds(rim + block, size)

    def copies(kind, src, dst, width, geometry):
        rim_x, block_x, rim_y, block_y = geometry
        out = []
        for k, (dx, dy) in enumerate(DIRS):
            sx, tx = cut(dx, width, rim_x, block_x)
            sy, ty = cut(dy, 8, rim_y, block_y)
            copy = pltpu.make_async_remote_copy(
                src_ref=src.at[sx, sy],
                dst_ref=dst.at[tx, ty],
                send_sem=send_sem.at[kind, k],
                recv_sem=recv_sem.at[kind, k],
                device_id=(me_x + dx, me_y + dy),
                device_id_type=MESH,
            )
            out.append((dx, dy, copy))
        return out

    def go(group):
        for dx, dy, copy in group:
            pl.when(inside(dx, dy))(copy.start)

    def arrive(group):
        for dx, dy, copy in group:
            pl.when(inside(-dx, -dy))(copy.wait_recv)

    def sent(group):
        for dx, dy, copy in group:
            pl.when(inside(dx, dy))(copy.wait_send)

    e0, f0, e1, f1 = refs["e0"], refs["f0"], refs["e1"], refs["f1"]
    vh0, vh1 = refs["vh0"], refs["vh1"]
    g0, g1 = (l0.rim_x, l0.block_x, l0.rim_y, l0.block_y), (l1.rim_x, l1.block_x, l1.rim_y, l1.block_y)
    p0, p1 = (l0.rim_pairs + 1, l0.block_pairs) + g0[2:], (l1.rim_pairs + 1, l1.block_pairs) + g1[2:]
    deep = 2 * SMOOTH
    send_e0 = copies(0, e0, e0, deep + 1, g0)
    send_f0 = copies(1, f0, f0, deep, g0)
    send_e1 = copies(2, e1, e1, deep + 2, g1)
    send_f1 = copies(3, f1, f1, deep + 1, g1)
    send_v0, send_v1 = [], []
    for c in range(2):
        send_v0 += copies(4 + c, l0.v[c], vh0.at[c], deep // 2, p0)
        send_v1 += copies(6 + c, l1.v[c], vh1.at[c], deep // 2 + 1, p1)

    x0, y0 = pl.ds(l0.rim_x, l0.block_x), pl.ds(l0.rim_y, l0.block_y)
    load_e = pltpu.make_async_copy(permit_ref, e0.at[x0, y0, :], local.at[0])
    load_f = pltpu.make_async_copy(right_ref, f0.at[x0, y0, :], local.at[1])
    load_e.start()
    load_f.start()

    def fill(ref, lead, value, geometry):
        rim_x, block_x, rim_y, block_y = geometry
        rows, high, width = ref.shape[-3:]
        top_x, top_y = rim_x + block_x, rim_y + block_y
        for xs, ys in (
            ((0, rim_x), (0, high)),
            ((top_x, rows), (0, high)),
            ((rim_x, top_x), (0, rim_y)),
            ((rim_x, top_x), (top_y, high)),
        ):
            part = jnp.full((xs[1] - xs[0], ys[1] - ys[0], width), value, F32)
            ref[lead + (slice(*xs), slice(*ys))] = part

    fill(e0, (), 1.0, g0)
    fill(f0, (), 0.0, g0)
    fill(e1, (), 1.0, g1)
    fill(f1, (), 0.0, g1)
    for c in range(2):
        fill(vh0, (c,), 0.0, p0)
        fill(vh1, (c,), 0.0, p1)
    barrier = pltpu.get_barrier_semaphore()

    def in_x(d):
        return (lax.rem(me_x + d, gx), me_y)

    def in_y(d):
        return (me_x, lax.rem(me_y + d, gy))

    def greet(to, count):
        def step(d, carry):
            pl.semaphore_signal(barrier, inc=1, device_id=to(d), device_id_type=MESH)
            return carry

        lax.fori_loop(1, count, step, 0)

    greet(in_x, gx)
    greet(in_y, gy)
    guests = jnp.int32(gx - 1 + gy - 1)
    for dx, dy in DIRS:
        if dx != 0 and dy != 0:

            @pl.when(inside(dx, dy))
            def _():
                pl.semaphore_signal(
                    barrier, inc=1, device_id=(me_x + dx, me_y + dy), device_id_type=MESH
                )

            guests = guests + inside(dx, dy).astype(jnp.int32)
    for level in (l0, l1):
        for c in range(2):
            for t in list(range(3)) + list(range(level.pairs - 1, level.pairs + 2)):
                level.v[c][t] = jnp.zeros((level.high, level.lanes), F32)
            for t in (0, level.pairs + 1):
                level.e[c][t] = jnp.ones((level.high, level.lanes), F32)
    pl.semaphore_wait(barrier, guests)

    load_e.wait()
    go(send_e0)
    load_f.wait()
    go(send_f0)

    tmp = refs["tmp"]
    lanes = l0.lanes

    def narrow(values, used, other):
        lane = iota(values.shape, len(values.shape) - 1)
        return jnp.where(lane < used, values, F32(other))

    put_rows(
        tmp,
        pl.ds(0, l1.block_x),
        e0[x0, y0, :].reshape(l1.block_x, 2, l0.block_y, lanes).sum(axis=1),
    )
    own_e1 = narrow(restrict(tmp, l1.block_x, l0.block_y), l1.zlen, 1.0)
    e1[pl.ds(l1.rim_x, l1.block_x), pl.ds(l1.rim_y, l1.block_y), :] = own_e1

    block2, z2 = l2.block_x, l2.zlen
    per = 128 // z2
    groups = block2 // per

    def gather_start(kind, rows):
        stage, packed = refs["stage"].at[kind], refs["packed"].at[kind]
        group = iota((8, 128), 1) // z2
        for g in range(groups):
            value = rows[g * per]
            for k in range(1, per):
                value = jnp.where(group == k, roll(rows[g * per + k], k * z2, 1), value)
            packed[g] = value
            stage[me_y, me_x, g] = value

        gather_line(kind, 0, in_x, gx, packed, stage.at[me_y, me_x])

    def gather_line(kind, stop, to, count, src, dst):
        def step(d, carry):
            pltpu.make_async_remote_copy(
                src_ref=src,
                dst_ref=dst,
                send_sem=all_send.at[kind, stop],
                recv_sem=all_recv.at[kind, stop],
                device_id=to(d),
                device_id_type=MESH,
            ).start()
            return carry

        lax.fori_loop(1, count, step, 0)

    def gather_next(kind):
        stage = refs["stage"].at[kind]
        others = stage.at[me_y, pl.ds(0, gx - 1)]
        pltpu.make_async_copy(others, others, all_recv.at[kind, 0]).wait()
        gather_line(kind, 1, in_y, gy, stage.at[me_y], stage.at[me_y])

    def gather_wait(kind, full):
        stage = refs["stage"].at[kind]
        others = stage.at[pl.ds(0, gy - 1)]
        pltpu.make_async_copy(others, others, all_recv.at[kind, 1]).wait()
        group = iota((8, 128), 1) // z2

        def step(q, _):
            for x in range(block2):
                tiles = []
                for h in range(full.shape[-1] // 128):
                    value = None
                    for k in range(per):
                        p = h * per + k
                        if p >= gx:
                            break
                        part = roll(stage[q, p, x // per], (k - x % per) * z2, 1)
                        value = part if k == 0 else jnp.where(group == k, part, value)
                    tiles.append(value)
                row = tiles[0] if len(tiles) == 1 else jnp.concatenate(tiles, axis=1)
                full[x, pl.ds(pl.multiple_of(q * 8 + 8, 8), 8), :] = row
            return 0

        lax.fori_loop(0, gy, step, 0)

    def gather_end(kind):
        others = refs["stage"].at[kind, 0, pl.ds(0, gx - 1)]
        pltpu.make_async_copy(others, others, all_send.at[kind, 0]).wait()
        others = refs["stage"].at[kind, pl.ds(0, gy - 1)]
        pltpu.make_async_copy(others, others, all_send.at[kind, 1]).wait()

    put_rows(tmp, pl.ds(0, block2), own_e1.reshape(block2, 2, l1.block_y, lanes).sum(axis=1))
    own_e2 = restrict(tmp, block2, l1.block_y)

    arrive([item for item in send_e0 if item[0] == 0])
    lo, hi = reach(l0, 0)
    ends = Ends(l0)
    pack(l0, lambda x: e0[x], put_e(l0), lo, hi)
    red_weights(l0, ends, lo + 1, hi - 1)
    black_weights(l0, ends, lo + 2, hi - 2)
    arrive([item for item in send_e0 if item[0] != 0])
    gather_start(0, own_e2)
    go(send_e1)
    far_lo, far_hi = reach(l0, deep)
    pack(l0, lambda x: e0[x], put_e(l0), 0, lo)
    pack(l0, lambda x: e0[x], put_e(l0), hi, l0.pairs)
    red_weights(l0, ends, far_lo - 1, lo + 1)
    red_weights(l0, ends, hi - 1, far_hi + 1)
    black_weights(l0, ends, far_lo, lo + 2)
    black_weights(l0, ends, hi - 2, far_hi)
    arrive(send_f0)
    gather_next(0)
    start(l0, lambda x: f0[x], deep - 1, deep)
    sweeps(l0, SMOOTH - 1, 1)
    residual_sums(l0, tmp)
    f1[pl.ds(l1.rim_x, l1.block_x), pl.ds(l1.rim_y, l1.block_y), :] = restrict(
        tmp, l1.block_x, l0.block_y
    )
    go(send_f1)

    arrive(send_e1)
    pack(l1, lambda x: e1[x], put_e(l1), 0, l1.pairs)
    coefficients(l1, deep)
    def coarse_permittivity(fine, coarse):
        for c in range(2):
            wrap(fine, fine.e[c])
        coefficients(fine, 0)
        for t in range(fine.pairs):
            put_rows(big, t, fine.e[0][t + 1] + fine.e[1][t + 1])
        rows = narrow(restrict(big, fine.pairs, fine.high), gx * coarse.zlen, 1.0)
        coarse.full[...] = rows
        pack(coarse, lambda x: coarse.full[x], put_e(coarse), 0, coarse.pairs)

    full, big = refs["full"], refs["big"]
    full[...] = jnp.zeros(full.shape, F32)
    gather_wait(0, full)
    pack(l2, lambda x: full[x, 8 : 8 + l2.high], put_e(l2), 0, l2.pairs)
    coarse_permittivity(l2, l3)

    arrive(send_f1)
    start(l1, lambda x: f1[x], deep - 1, deep + 1)
    sweeps(l1, SMOOTH - 1, 1)
    residual_sums(l1, tmp)
    gather_start(1, restrict(tmp, block2, l1.block_y))
    coarse_permittivity(l3, l4)
    gather_next(1)
    for c in range(2):
        wrap(l4, l4.e[c])
    coefficients(l4, 0)

    gather_wait(1, full)
    go(send_v1)
    go(send_v0)
    start(l2, lambda x: full[x, 8 : 8 + l2.high], 0, 0)
    sweeps(l2, SMOOTH - 1, 0)
    for fine, coarse in ((l2, l3), (l3, l4)):
        residual_sums(fine, big)
        coarse.full[...] = restrict(big, fine.pairs, fine.high)
        small = coarse is l4 and coarse.pairs == 1
        start(coarse, lambda x: coarse.full[x], None if small else 0, 0)
        if small:
            solve_small(coarse, COARSE_SWEEPS)
        else:
            sweeps(coarse, SMOOTH - 1 if coarse is l3 else COARSE_SWEEPS - 1, 0)

    def correct(fine, coarse):
        s = even_mask(coarse.high, coarse.lanes)
        spread(big, jnp.stack([coarse_row(coarse, s, t) for t in range(fine.pairs)]))
        for c in range(2):
            for t in range(fine.pairs):
                fine.v[c][t + 1] = fine.v[c][t + 1] + get_row(big, t, fine.high)
            wrap_values(fine, c)
        sweeps(fine, SMOOTH, 0)

    correct(l3, l4)
    correct(l2, l3)

    def add(level, halo, far_lo, far_hi):
        lo, hi = reach(level, 0)
        ylo, yhi = level.rim_y, level.rim_y + level.block_y
        for c in range(2):
            for t in list(range(far_lo, lo)) + list(range(hi, far_hi)):
                level.v[c][t + 1] = halo[c, t + 1] + get_row(tmp, t - far_lo, level.high)

            def step(t):
                row = jnp.concatenate(
                    [
                        halo[c, t + 1, 0:ylo],
                        level.v[c][t + 1, ylo:yhi],
                        halo[c, t + 1, yhi : level.high],
                    ],
                    axis=0,
                )
                level.v[c][t + 1] = row + get_row(tmp, t - far_lo, level.high)

            loop(level, lo, hi, step)

    s2 = even_mask(l2.high, l2.lanes)
    for x in range(block2):
        full[x, 8 : 8 + l2.high, :] = coarse_row(l2, s2, x)
    rows = []
    high = l1.high // 2
    skip = 8 - l1.rim_y // 2
    for t in range(l1.pairs):
        x = t - l1.rim_pairs
        p = lax.rem(me_x + x // block2 + gx, gx)
        value = full[x % block2, pl.ds(pl.multiple_of(me_y * 8, 8), 24), :]
        value = pltpu.roll(value, lax.rem(l2.lanes - p * z2, l2.lanes), 1)
        rows.append(value[skip : skip + high, 0:128])
    arrive(send_v1)
    sent(send_v1)
    spread(tmp, jnp.stack(rows))
    add(l1, vh1, 0, l1.pairs)
    sweeps(l1, SMOOTH, 2)

    s1 = even_mask(l1.high, l1.lanes)
    first = l1.rim_x - l0.rim_pairs
    low = l1.rim_y - l0.rim_y // 2
    far_lo, far_hi = reach(l0, deep)
    rows = [coarse_row(l1, s1, first + t)[low : low + l0.high // 2] for t in range(far_lo, far_hi)]
    arrive(send_v0)
    sent(send_v0)
    spread(tmp, jnp.stack(rows))
    add(l0, vh0, far_lo, far_hi)
    sweeps(l0, SMOOTH, 0)

    s0 = even_mask(l0.high, l0.lanes)

    def last(t):
        red, black = l0.v[0][t + l0.rim_pairs + 1], l0.v[1][t + l0.rim_pairs + 1]
        lo, hi = l0.rim_y, l0.rim_y + l0.block_y
        out_ref[2 * t] = jnp.where(s0, red, black)[lo:hi]
        out_ref[2 * t + 1] = jnp.where(s0, black, red)[lo:hi]

    loop(l0, 0, l0.block_pairs, last)
    for group in (send_e0, send_f0, send_e1, send_f1):
        sent(group)
    for kind in range(2):
        gather_end(kind)


def per_device(gx, gy, right_side, permittivity):
    bx, by, nz = right_side.shape
    wide = -(-gx * (nz // 4) // 128) * 128
    scratch, names = [], []

    def buffer(owner, name, *shape):
        scratch.append(pltpu.VMEM(shape, F32))
        names.append((owner, name))

    refs = {}
    levels = []
    for index in range(LEVELS):
        level = Level()
        level.index, level.gx = index, gx
        level.zlen = nz >> index
        level.whole = index >= 2
        level.block_x = bx >> index
        if level.whole:
            level.rim_x = level.rim_y = level.rim_pairs = 0
            level.pairs = level.block_pairs = level.block_x // 2
            level.high = level.block_y = (by >> index) * gy
            level.lanes = wide
        else:
            level.rim_x, level.rim_y = 6, 8
            level.block_y = by >> index
            level.rim_pairs, level.block_pairs = level.rim_x // 2, level.block_x // 2
            level.pairs = level.block_pairs + 2 * level.rim_pairs
            level.high = level.block_y + 2 * level.rim_y
            level.lanes = nz
        size = (level.high, level.lanes)
        level.e, level.v = [None, None], [None, None]
        for c in range(2):
            buffer(level.e, c, level.pairs + 2, *size)
            buffer(level.v, c, level.pairs + 2, *size)
        level.straight = level.whole and level.pairs * level.high * level.lanes <= 32 * 1024
        buffer(level, "inv", 2, level.pairs, *size)
        buffer(level, "a", 2, 6, level.pairs, *size)
        if index < 2:
            buffer(None, f"e{index}", 2 * level.pairs, *size)
            buffer(None, f"f{index}", 2 * level.pairs, *size)
            buffer(None, f"vh{index}", 2, level.pairs + 2, *size)
        if index == 2:
            buffer(None, "big", level.pairs, level.lanes // 128, level.high, 128)
            buffer(None, "full", level.block_x, level.high + 16, level.lanes)
        if index > 2:
            buffer(level, "full", level.block_x, *size)
        levels.append(level)
    l0 = levels[0]
    buffer(None, "tmp", l0.pairs, 1, l0.high, l0.lanes)
    groups = levels[2].block_x // (128 // levels[2].zlen)
    buffer(None, "stage", 2, gy, gx, groups, 8, 128)
    buffer(None, "packed", 2, groups, 8, 128)
    sems = [
        pltpu.SemaphoreType.DMA((8, 8)),
        pltpu.SemaphoreType.DMA((8, 8)),
        pltpu.SemaphoreType.DMA((2, 2)),
        pltpu.SemaphoreType.DMA((2, 2)),
        pltpu.SemaphoreType.DMA((2,)),
    ]

    def body(right_ref, permit_ref, out_ref, *buffers):
        me_x, me_y = lax.axis_index("gx"), lax.axis_index("gy")
        for (owner, name), ref in zip(names, buffers):
            if owner is None:
                refs[name] = ref
            elif isinstance(owner, list):
                owner[name] = ref
            else:
                setattr(owner, name, ref)
        refs["sems"] = buffers[len(names) :]
        for level in levels:
            if level.whole:
                level.first_x, level.last_x = 0, level.pairs - 1
                level.first_y, level.last_y = 0, level.high - 1
            else:
                level.first_x = level.rim_pairs - me_x * level.block_pairs
                level.last_x = level.first_x + gx * level.block_pairs - 1
                level.first_y = level.rim_y - me_y * level.block_y
                level.last_y = level.first_y + gy * level.block_y - 1
        kernel(gx, gy, right_ref, permit_ref, out_ref, refs, levels)

    return pl.pallas_call(
        body,
        out_shape=jax.ShapeDtypeStruct(right_side.shape, F32),
        in_specs=[pl.BlockSpec(memory_space=pl.ANY)] * 2,
        out_specs=pl.BlockSpec(memory_space=pltpu.VMEM),
        scratch_shapes=scratch + sems,
        compiler_params=pltpu.CompilerParams(
            collective_id=0, has_side_effects=True, vmem_limit_bytes=60 * 2**20
        ),
    )(right_side, permittivity)


def solution(mesh):
    gx, gy = mesh.shape["gx"], mesh.shape["gy"]
    placed = (P("gx", "gy", None), P("gx", "gy", None))
    return jax.shard_map(
        functools.partial(per_device, gx, gy),
        mesh=mesh,
        in_specs=placed,
        out_specs=P("gx", "gy", None),
        check_vma=False,
    )
```
